32 devices in a mesh: seq: 8 (over z, y), doc: 4 (over x, core).
Axes of the slice: x: 2, y: 2, z: 4, core: 2. Of those that a mesh axis runs over, the one named last changes fastest.
Arguments:
- byte_q: bfloat16 [16384, 1024], P(('doc', 'seq')), parts along dimension 0, may hold values from -6 to 6
- byte_k: bfloat16 [16384, 1024], P(('doc', 'seq')), parts along dimension 0, may hold values from -6 to 6
- byte_v: bfloat16 [16384, 1024], P(('doc', 'seq')), parts along dimension 0, may hold values from -6 to 6
- byte_gain: bfloat16 [1024], replicated, may hold values from 0.2 to 4.5
- pool_query: bfloat16 [8, 128], replicated, may hold values from -12 to 12
- w_up: bfloat16 [1024, 2048], P('seq'), may hold values from -1 to 1
- patch_gain: bfloat16 [2048], replicated, may hold values from 0.099609375 to 1.8984375
- w_kv: bfloat16 [2048, 1024], P('seq'), may hold values from -1 to 1
- out_gain: bfloat16 [2048], replicated, may hold values from 0.2 to 4.5
- dec_gain: bfloat16 [1024], replicated, may hold values from 0.099609375 to 1.8984375
- patch_start: int32 [32, 80], P('doc'), parts along dimension 0, may hold values from 0 to 512, as said below
Outputs:
- byte_out: bfloat16 [16384, 1024], P(('doc', 'seq')), parts along dimension 0
- patch_out: bfloat16 [2560, 2048], P(('doc', 'seq')), parts along dimension 0
The draws below stay inside these ranges and needn't reach their ends.
There are 4 independent parts, one for each index of `doc`. The reference program is written for one: setup_inputs(seed, part) draws one part's arguments, and reference() takes and returns one part's arrays. A program takes and returns all parts, laid end to end along the dimension named above; an argument that names none is the same for every part. Nothing has to cross between parts.
Inputs may be any that keep to these rules, and one draw needn't show every extreme that they name: `patch_start`: row r lists the patch starts of block r: 0 first, strictly rising over its live slots, then 512 in every unused slot; each row has at least 20 live slots, and some row has all 80 live.
All inputs are finite; a program needn't handle non-finite values.
Results may differ from the reference program's by a relative error of at most 0.0085.
Values may be sent and summed in bfloat16 or wider, within the bound.
No kernel may reach another device: no remote copies, remote signals or barrier semaphores. Data moves between devices by JAX's collectives and lax.ppermute only.
A program may use at most 128 MiB of HBM per device.

```python
import jax
import jax.numpy as jnp
from jax import lax

D = 1024
HB = 8
HD = 128
PATCH_WIDTH = 2048
PATCH_QUERY_HEADS = 32
PATCH_KEY_HEADS = 8
PATCH_HEAD_SIZE = 64
WINDOW = 512
BYTES_DEV = 512
PATCH_SLOTS = 80
LENGTH = 4096
N_SEQ = 8


def standard_gaussian(key, salt, shape, scale, bound):
    values = jax.random.normal(jax.random.fold_in(key, salt), shape, jnp.float32) * scale
    return jnp.clip(values, -bound, bound)


def draw_byte_q(key, part):
    return standard_gaussian(key, 23, (LENGTH, D), 1.0, 6.0).astype(jnp.bfloat16)


def draw_byte_k(key, part):
    return standard_gaussian(key, 24, (LENGTH, D), 1.0, 6.0).astype(jnp.bfloat16)


def draw_byte_v(key, part):
    return standard_gaussian(key, 25, (LENGTH, D), 1.0, 6.0).astype(jnp.bfloat16)


def draw_byte_gain(key, part):
    return (1.0 + 0.18 * standard_gaussian(key, 27, (D,), 1.0, 4.4)).astype(jnp.bfloat16)


def draw_out_gain(key, part):
    return (1.0 + 0.18 * standard_gaussian(key, 29, (PATCH_WIDTH,), 1.0, 4.4)).astype(jnp.bfloat16)


def draw_pool_query(key, part):
    return standard_gaussian(key, 31, (HB, HD), 2.0, 12.0).astype(jnp.bfloat16)


def draw_w_up(key, part):
    random_jitter = standard_gaussian(key, 32, (D, PATCH_WIDTH), 1.0, 4.0) * D ** (-0.5)
    return random_jitter.astype(jnp.bfloat16)


def draw_w_kv(key, part):
    random_jitter = standard_gaussian(key, 33, (PATCH_WIDTH, 2 * PATCH_KEY_HEADS * PATCH_HEAD_SIZE), 1.0, 4.0) * PATCH_WIDTH ** (-0.5)
    return random_jitter.astype(jnp.bfloat16)


def draw_patch_start(key, part):
    count_key = jax.random.fold_in(key, 11)
    full_key = jax.random.fold_in(key, 12)
    place_key = jax.random.fold_in(key, 13)
    counts = jax.random.randint(count_key, (N_SEQ,), PATCH_SLOTS // 4, PATCH_SLOTS + 1)
    full_row = jax.random.randint(full_key, (), 0, N_SEQ)
    counts = jnp.where(jnp.arange(N_SEQ) == full_row, PATCH_SLOTS, counts)
    row_keys = jax.random.split(place_key, N_SEQ)

    def one_row(row_key, live_count):
        shuffled = jax.random.permutation(row_key, BYTES_DEV - 1) + 1
        places = jnp.arange(BYTES_DEV - 1)
        chosen = jnp.where(places < live_count - 1, shuffled, BYTES_DEV)
        ordered = jnp.sort(chosen)[:PATCH_SLOTS - 1]
        return jnp.concatenate([jnp.zeros((1,), jnp.int32), ordered.astype(jnp.int32)])
    return jax.vmap(one_row)(row_keys, counts).astype(jnp.int32)


def setup_inputs(seed: int = 0, part: int = 0) -> dict:
    splits = jax.random.split(jax.random.key(seed), 12)
    part_splits = jax.random.split(jax.random.fold_in(splits[11], part), 12)
    byte_q = draw_byte_q(jax.random.fold_in(jax.random.fold_in(splits[11], part), 71), part)
    byte_k = draw_byte_k(jax.random.fold_in(jax.random.fold_in(splits[11], part), 71), part)
    byte_v = draw_byte_v(jax.random.fold_in(jax.random.fold_in(splits[11], part), 71), part)
    byte_gain = draw_byte_gain(jax.random.fold_in(splits[11], 71), part)
    pool_query = draw_pool_query(jax.random.fold_in(splits[11], 71), part)
    w_up = draw_w_up(jax.random.fold_in(splits[11], 71), part)
    patch_gain = jnp.clip(1.0 + 0.18 * jax.random.normal(splits[6], (PATCH_WIDTH,), jnp.float32), 0.099609375, 1.8984375).astype(jnp.bfloat16)
    w_kv = draw_w_kv(jax.random.fold_in(splits[11], 71), part)
    out_gain = draw_out_gain(jax.random.fold_in(splits[11], 71), part)
    dec_gain = jnp.clip(1.0 + 0.18 * jax.random.normal(splits[9], (D,), jnp.float32), 0.099609375, 1.8984375).astype(jnp.bfloat16)
    patch_start = draw_patch_start(jax.random.fold_in(jax.random.fold_in(splits[11], part), 71), part)
    return dict(byte_q=byte_q, byte_k=byte_k, byte_v=byte_v, byte_gain=byte_gain, pool_query=pool_query, w_up=w_up, patch_gain=patch_gain, w_kv=w_kv, out_gain=out_gain, dec_gain=dec_gain, patch_start=patch_start)


epsilon = 1e-06

def normed(matrix, gains):
    matrix = matrix.astype(jnp.float32)
    return matrix * lax.rsqrt(lax.optimization_barrier(jnp.mean(matrix * matrix, axis=-1, keepdims=True)) + epsilon) * gains.astype(jnp.float32)

def softmax_rows(scores, allowed):
    scores = jnp.where(allowed, scores, -jnp.inf)
    peak = lax.optimization_barrier(jnp.max(scores, axis=-1, keepdims=True))
    expo = jnp.where(allowed, jnp.exp(scores - peak), 0.0)
    return (expo / lax.optimization_barrier(jnp.sum(expo, axis=-1, keepdims=True))).astype(jnp.bfloat16)

def byte_block(query_rows, key_rows, value_rows, leading):
    nbytes = query_rows.shape[0]
    reach = key_rows.shape[0] - nbytes
    query_head_rows = query_rows.astype(jnp.float32).reshape(nbytes, HB, HD)
    key_head_rows = key_rows.astype(jnp.float32).reshape(nbytes + reach, HB, HD)
    value_head_rows = value_rows.astype(jnp.float32).reshape(nbytes + reach, HB, HD)
    scores = jnp.einsum('qhd,khd->hqk', query_head_rows, key_head_rows) * HD ** (-0.5)
    row_pos = jnp.arange(nbytes, dtype=jnp.int32)[:, None]
    col_pos = jnp.arange(nbytes + reach, dtype=jnp.int32)[None, :]
    allowed = (col_pos > row_pos) & (col_pos <= row_pos + reach) & ((col_pos >= reach) | jnp.logical_not(leading))
    weights = softmax_rows(scores, allowed[None])
    mixed = jnp.einsum('hqk,khd->qhd', weights.astype(jnp.float32), value_head_rows)
    return mixed.reshape(nbytes, HB * HD)

def segments(starts, nbytes):
    positions = jnp.arange(nbytes, dtype=jnp.int32)
    segment = (lax.optimization_barrier(jnp.sum((starts[None, :] <= positions[:, None]).astype(jnp.int32), axis=1)) - 1).astype(jnp.int32)
    member = segment[None, :] == jnp.arange(starts.shape[0], dtype=jnp.int32)[:, None]
    return (segment, member)

def pool(encoded, starts, pool_query):
    nbytes = encoded.shape[0]
    segment, member = segments(starts, nbytes)
    enc_heads = encoded.astype(jnp.float32).reshape(nbytes, HB, HD)
    scores = jnp.einsum('bhd,hd->bh', enc_heads, pool_query.astype(jnp.float32)) * HD ** (-0.5)
    inside = member[:, :, None]
    highest = lax.optimization_barrier(jnp.max(jnp.where(inside, scores[None], -jnp.inf), axis=1))
    own_max = lax.optimization_barrier(jnp.max(jnp.where(inside, highest[:, None, :], -jnp.inf), axis=0))
    expo = jnp.exp(scores - own_max)
    totals = lax.optimization_barrier(jnp.sum(jnp.where(inside, expo[None], 0.0), axis=1))
    divisor = lax.optimization_barrier(jnp.max(jnp.where(inside, totals[:, None, :], 0.0), axis=0))
    weights = (expo / divisor).astype(jnp.bfloat16)
    spread = jnp.where(inside, weights[None], jnp.zeros((), jnp.bfloat16))
    pooled = jnp.einsum('pbh,bhd->phd', spread.astype(jnp.float32), enc_heads)
    return pooled.reshape(starts.shape[0], HB * HD).astype(jnp.bfloat16)

def patch_block(query_rows, key_value_pairs, query_start, is_live):
    slot_total_count = query_rows.shape[0]
    overall_row_count = key_value_pairs.shape[0]
    head_groups = PATCH_QUERY_HEADS // PATCH_KEY_HEADS
    query_head_rows = query_rows.astype(jnp.float32).reshape(slot_total_count, PATCH_KEY_HEADS, head_groups, PATCH_HEAD_SIZE)
    key_head_rows = key_value_pairs[:, :PATCH_KEY_HEADS * PATCH_HEAD_SIZE].astype(jnp.float32).reshape(overall_row_count, PATCH_KEY_HEADS, PATCH_HEAD_SIZE)
    value_head_rows = key_value_pairs[:, PATCH_KEY_HEADS * PATCH_HEAD_SIZE:].astype(jnp.float32).reshape(overall_row_count, PATCH_KEY_HEADS, PATCH_HEAD_SIZE)
    scores = jnp.einsum('qkgd,pkd->kgqp', query_head_rows, key_head_rows) * PATCH_HEAD_SIZE ** (-0.5)
    query_pos = query_start + jnp.arange(slot_total_count, dtype=jnp.int32)
    key_pos = jnp.arange(overall_row_count, dtype=jnp.int32)
    allowed = (key_pos[None, :] <= query_pos[:, None]) & is_live[None, :]
    weights = softmax_rows(scores, allowed[None, None])
    mixed = jnp.einsum('kgqp,pkd->qkgd', weights.astype(jnp.float32), value_head_rows)
    return mixed.reshape(slot_total_count, PATCH_QUERY_HEADS * PATCH_HEAD_SIZE)

def decode(encoded, patch_rows, starts):
    nbytes = encoded.shape[0]
    slot_total_count = patch_rows.shape[0]
    segment, member = segments(starts, nbytes)
    enc_heads = encoded.astype(jnp.float32).reshape(nbytes, HB, HD)
    packed = patch_rows.astype(jnp.float32).reshape(slot_total_count, HB, 2, HD)
    scores = jnp.einsum('bhd,phd->hbp', enc_heads, packed[:, :, 0]) * HD ** (-0.5)
    allowed = jnp.arange(slot_total_count, dtype=jnp.int32)[None, :] <= segment[:, None]
    weights = softmax_rows(scores, allowed[None])
    mixed = jnp.einsum('hbp,phd->bhd', weights.astype(jnp.float32), packed[:, :, 1])
    return mixed.reshape(nbytes, HB * HD)

def reference(byte_q, byte_k, byte_v, byte_gain, pool_query, w_up, patch_gain, w_kv, out_gain, dec_gain, patch_start):
    reach = WINDOW
    nbytes = BYTES_DEV
    blank = jnp.zeros((reach, D), byte_k.dtype)
    key_padded = jnp.concatenate([blank, byte_k], axis=0)
    value_padded = jnp.concatenate([blank, byte_v], axis=0)

    def encode_one(device):
        query_rows = lax.dynamic_slice_in_dim(byte_q, device * nbytes, nbytes, 0)
        key_rows = lax.dynamic_slice_in_dim(key_padded, device * nbytes, reach + nbytes, 0)
        value_rows = lax.dynamic_slice_in_dim(value_padded, device * nbytes, reach + nbytes, 0)
        return normed(byte_block(query_rows, key_rows, value_rows, device == 0), byte_gain).astype(jnp.bfloat16)
    devices = jnp.arange(N_SEQ, dtype=jnp.int32)
    encoded = lax.map(encode_one, devices)
    pooled = lax.map(lambda operands: pool(operands[0], operands[1], pool_query), (encoded, patch_start))
    lifted = jnp.dot(pooled.reshape(N_SEQ * PATCH_SLOTS, D), w_up, preferred_element_type=jnp.float32)
    patch_input = normed(lifted, patch_gain).astype(jnp.bfloat16)
    key_value_pairs = jnp.dot(patch_input, w_kv, preferred_element_type=jnp.float32).astype(jnp.bfloat16)
    counts = lax.optimization_barrier(jnp.sum((patch_start < nbytes).astype(jnp.int32), axis=1))
    live_grid = jnp.arange(PATCH_SLOTS, dtype=jnp.int32)[None, :] < counts[:, None]
    is_live = live_grid.reshape(N_SEQ * PATCH_SLOTS)

    def attend_one(device):
        query_rows = lax.dynamic_slice_in_dim(patch_input, device * PATCH_SLOTS, PATCH_SLOTS, 0)
        mixed = patch_block(query_rows, key_value_pairs, device * PATCH_SLOTS, is_live)
        alive = lax.dynamic_index_in_dim(live_grid, device, 0, keepdims=False)
        return (normed(mixed, out_gain) * alive[:, None].astype(jnp.float32)).astype(jnp.bfloat16)
    patch_out = lax.map(attend_one, devices)

    def decode_one(operands):
        return normed(decode(operands[0], operands[1], operands[2]), dec_gain).astype(jnp.bfloat16)
    byte_out = lax.map(decode_one, (encoded, patch_out, patch_start))
    return (byte_out.reshape(N_SEQ * nbytes, D), patch_out.reshape(N_SEQ * PATCH_SLOTS, PATCH_QUERY_HEADS * PATCH_HEAD_SIZE))
```

```python
import functools

import jax
import jax.numpy as jnp
from jax import lax
from jax.experimental import pallas as pl
from jax.experimental.pallas import tpu as pltpu
from jax.sharding import PartitionSpec as P

PATCH_QUERY_HEADS = 32
PATCH_KEY_HEADS = 8
LOG2E = 1.4426950408889634
LOW = -1e30
TILE = 128
epsilon = 1e-06
VMEM = pl.BlockSpec(memory_space=pltpu.VMEM)
ANY = pl.BlockSpec(memory_space=pl.ANY)


def dot_t(a, b):
    return lax.dot_general(a, b, (((1,), (1,)), ((), ())), preferred_element_type=jnp.float32)


def dot(a, b):
    return jnp.dot(a, b, preferred_element_type=jnp.float32)


def own_kernel(q_ref, k_ref, v_ref, mix_ref, lse_ref):
    head = pl.program_id(0)
    nbytes, size = q_ref.shape
    factor = size ** (-0.5) * LOG2E
    row = lax.broadcasted_iota(jnp.int32, (TILE, TILE), 0)
    col = lax.broadcasted_iota(jnp.int32, (TILE, TILE), 1)
    causal = col <= row
    values = jnp.concatenate([v_ref[...], jnp.ones((nbytes, size), jnp.bfloat16)], axis=1)
    lane = lax.broadcasted_iota(jnp.int32, (TILE, TILE), 1)

    for start in range(0, nbytes, TILE):
        end = start + TILE
        scores = dot_t(q_ref[start:end, :], k_ref[:end, :])
        last = jnp.where(causal, scores[:, start:end], LOW)
        scores = last if start == 0 else jnp.concatenate([scores[:, :start], last], axis=1)
        peak = jnp.max(scores, axis=1, keepdims=True)
        expo = jnp.exp2((scores - peak) * factor).astype(jnp.bfloat16)
        total = dot(expo, values[:end])
        mix_ref[start:end, :] = total[:, :size] / total[:, size:]
        lse = peak * factor + jnp.log2(total[:, size:])
        lse_ref[start:end, :] = jnp.where(lane == head, lse, lse_ref[start:end, :])


def own_attention(q, k, v):
    nbytes, width = q.shape
    block = pl.BlockSpec((nbytes, TILE), lambda h: (0, h))
    return pl.pallas_call(
        own_kernel,
        grid=(width // TILE,),
        in_specs=[block] * 3,
        out_specs=[block, pl.BlockSpec((nbytes, TILE), lambda h: (0, 0))],
        out_shape=[
            jax.ShapeDtypeStruct((nbytes, width), jnp.float32),
            jax.ShapeDtypeStruct((nbytes, TILE), jnp.float32),
        ],
        compiler_params=pltpu.CompilerParams(vmem_limit_bytes=24 * 2**20),
        name="own_attention",
    )(q, k, v)


def cross_kernel(
    lead_ref, q_ref, k_ref, v_ref, own_ref, lse_ref, gain_ref, query_ref, start_ref, next_ref,
    enc_ref, pooled_ref, mix_ref,
):
    head = pl.program_id(0)
    heads = pl.num_programs(0)
    nbytes, size = q_ref.shape
    slots = start_ref.shape[0]
    width = mix_ref.shape[1]
    factor = size ** (-0.5) * LOG2E
    row = lax.broadcasted_iota(jnp.int32, (TILE, TILE), 0)
    col = lax.broadcasted_iota(jnp.int32, (TILE, TILE), 1)
    later = (col > row) & (lead_ref[0] == 0)
    bias = jnp.where(lead_ref[0] == 0, 0.0, LOW)
    values = jnp.concatenate([v_ref[...], jnp.ones((nbytes, size), jnp.bfloat16)], axis=1)
    lane = lax.broadcasted_iota(jnp.int32, (TILE, TILE), 1)

    for start in range(0, nbytes, TILE):
        end = start + TILE
        scores = dot_t(q_ref[start:end, :], k_ref[start:, :])
        first = jnp.where(later, scores[:, :TILE], LOW)
        if end < nbytes:
            scores = jnp.concatenate([first, scores[:, TILE:] + bias], axis=1)
        else:
            scores = first
        lse = jnp.sum(jnp.where(lane == head, lse_ref[start:end, :], 0.0), axis=1, keepdims=True)
        peak = jnp.maximum(jnp.max(scores, axis=1, keepdims=True) * factor, lse)
        expo = jnp.exp2(scores * factor - peak).astype(jnp.bfloat16)
        total = dot(expo, values[start:])
        share = jnp.exp2(lse - peak)
        columns = pl.ds(pl.multiple_of(head * size, size), size)
        mix_ref[start:end, columns] = (own_ref[start:end, :] * share + total[:, :size]) / (
            share + total[:, size:]
        )

    @pl.when(head == heads - 1)
    def _():
        for start in range(0, nbytes, TILE):
            end = start + TILE
            mix = mix_ref[start:end, :]
            scale = lax.rsqrt(jnp.mean(mix * mix, axis=1, keepdims=True) + epsilon)
            enc_ref[start:end, :] = (mix * scale * gain_ref[...]).astype(jnp.bfloat16)
        enc = enc_ref[...]
        n_heads = query_ref.shape[0]
        wide = jnp.concatenate([query_ref[...].astype(jnp.float32)] * n_heads, axis=1)
        head_row = lax.broadcasted_iota(jnp.int32, wide.shape, 0)
        head_col = lax.broadcasted_iota(jnp.int32, wide.shape, 1) // size
        wide = jnp.where(head_row == head_col, wide, 0.0).astype(jnp.bfloat16)
        scores = dot_t(wide, enc) * factor
        place = lax.broadcasted_iota(jnp.int32, (slots, nbytes), 1)
        member = (place >= start_ref[...]) & (place < next_ref[...])
        for h in range(n_heads):
            inside = jnp.where(member, scores[h : h + 1, :], LOW)
            peak = jnp.max(inside, axis=1, keepdims=True)
            expo = jnp.where(member, jnp.exp2(inside - peak), 0.0)
            total = jnp.sum(expo, axis=1, keepdims=True)
            weights = (expo * jnp.where(total > 0, 1.0 / total, 0.0)).astype(jnp.bfloat16)
            pooled_ref[:, h * size : (h + 1) * size] = dot(
                weights, enc[:, h * size : (h + 1) * size]
            ).astype(jnp.bfloat16)


def cross_attention(leading, q, k, v, own, lse, gain, pool_query, starts, ends):
    nbytes, width = q.shape
    slots = starts.shape[0]
    block = pl.BlockSpec((nbytes, TILE), lambda h: (0, h))

    def whole(*shape):
        return pl.BlockSpec(shape, lambda h: (0,) * len(shape))

    return pl.pallas_call(
        cross_kernel,
        grid=(width // TILE,),
        in_specs=[
            pl.BlockSpec(memory_space=pltpu.SMEM),
            block,
            block,
            block,
            block,
            whole(nbytes, TILE),
            whole(1, width),
            whole(*pool_query.shape),
            whole(slots, 1),
            whole(slots, 1),
        ],
        out_specs=[whole(nbytes, width), whole(slots, width)],
        out_shape=[
            jax.ShapeDtypeStruct((nbytes, width), jnp.bfloat16),
            jax.ShapeDtypeStruct((slots, width), jnp.bfloat16),
        ],
        scratch_shapes=[pltpu.VMEM((nbytes, width), jnp.float32)],
        compiler_params=pltpu.CompilerParams(vmem_limit_bytes=32 * 2**20),
        name="cross_attention",
    )(leading, q, k, v, own, lse, gain, pool_query, starts, ends)


def patch_kernel(n_blocks, plan, n_weights, at_ref, *refs):
    blocks = refs[:n_blocks]
    weights = refs[n_blocks : n_blocks + n_weights]
    (
        enc_ref, bias_ref, pgain_ref, ogain_ref, dgain_ref, start_col_ref, start_row_ref,
        byte_ref, patch_ref, up_ref, kv_w_ref, kv_ref, mix_ref, in_ref, sems,
    ) = refs[n_blocks + n_weights :]
    copies = plan(at_ref, weights, up_ref, kv_w_ref)
    copies = [
        pltpu.make_async_copy(source, target, sems.at[i]) for i, (source, target) in enumerate(copies)
    ]
    for copy in copies:
        copy.start()
    for copy in copies:
        copy.wait()

    slots = patch_ref.shape[0]
    offset = 0
    for b, block in enumerate(blocks):
        rows = block.shape[0]
        step = rows if rows <= 4 * slots else 4 * slots
        for r in range(0, rows, step):
            lifted = dot(block[r : r + step, :], up_ref[...])
            scale = lax.rsqrt(jnp.mean(lifted * lifted, axis=1, keepdims=True) + epsilon)
            patch_in = (lifted * scale * pgain_ref[...]).astype(jnp.bfloat16)
            if b == 0:
                in_ref[...] = patch_in[:slots]
            kv_ref[offset + r : offset + r + step, :] = dot(patch_in, kv_w_ref[...]).astype(
                jnp.bfloat16
            )
        offset += rows

    size = patch_ref.shape[1] // PATCH_QUERY_HEADS
    rows = kv_ref.shape[0]
    half_width = PATCH_KEY_HEADS * size
    factor = size ** (-0.5) * LOG2E
    groups = PATCH_QUERY_HEADS // PATCH_KEY_HEADS
    pair = 2 * size
    lane_half = lax.broadcasted_iota(jnp.int32, (slots, pair), 1) // size
    ones = jnp.ones((rows, pair), jnp.bfloat16)
    for kp in range(PATCH_KEY_HEADS // 2):
        keys = kv_ref[:, kp * pair : (kp + 1) * pair]
        values = jnp.concatenate(
            [kv_ref[:, half_width + kp * pair : half_width + (kp + 1) * pair], ones], axis=1
        )
        for half in range(2):
            first = (2 * kp + half) * groups
            queries = []
            for g in range(groups):
                at = (first + g) // 2 * pair
                q = in_ref[:, at : at + pair].astype(jnp.float32)
                if g % 2 != half:
                    q = pltpu.roll(q, size, 1)
                queries.append(jnp.where(lane_half == half, q, 0.0).astype(jnp.bfloat16))
            scores = dot_t(jnp.concatenate(queries, axis=0), keys)
            outs = []
            for g in range(groups):
                part = scores[g * slots : (g + 1) * slots, :] * factor + bias_ref[...]
                peak = jnp.max(part, axis=1, keepdims=True)
                outs.append(jnp.exp2(part - peak).astype(jnp.bfloat16))
            total = dot(jnp.concatenate(outs, axis=0), values)
            mixed = total[:, :pair] / total[:, pair:]
            for g in range(0, groups, 2):
                two = [mixed[(g + i) * slots : (g + i + 1) * slots, :] for i in range(2)]
                two = [t if i == half else pltpu.roll(t, size, 1) for i, t in enumerate(two)]
                at = (first + g) // 2 * pair
                mix_ref[:, at : at + pair] = jnp.where(lane_half == 0, two[0], two[1])

    nbytes = enc_ref.shape[0]
    mix = mix_ref[...]
    scale = lax.rsqrt(jnp.mean(mix * mix, axis=1, keepdims=True) + epsilon)
    alive = jnp.where(start_col_ref[...] < nbytes, 1.0, 0.0)
    patch_ref[...] = (mix * scale * ogain_ref[...] * alive).astype(jnp.bfloat16)

    width = enc_ref.shape[1]
    size = TILE
    factor = size ** (-0.5) * LOG2E
    ones = jnp.ones((slots, size), jnp.bfloat16)
    for start in range(0, nbytes, TILE):
        place = lax.broadcasted_iota(jnp.int32, (TILE, slots), 0) + start
        allowed = start_row_ref[...] <= place
        crosses = []
        squares = jnp.zeros((TILE, size), jnp.float32)
        for h in range(width // size):
            scores = dot_t(
                enc_ref[start : start + TILE, h * size : (h + 1) * size],
                patch_ref[:, 2 * h * size : (2 * h + 1) * size],
            )
            scores = jnp.where(allowed, scores * factor, LOW)
            peak = jnp.max(scores, axis=1, keepdims=True)
            expo = jnp.exp2(scores - peak).astype(jnp.bfloat16)
            values = jnp.concatenate(
                [patch_ref[:, (2 * h + 1) * size : (2 * h + 2) * size], ones], axis=1
            )
            total = dot(expo, values)
            cross = total[:, :size] / total[:, size:]
            squares += cross * cross
            crosses.append(cross)
        scale = lax.rsqrt(jnp.sum(squares, axis=1, keepdims=True) / width + epsilon)
        for h, cross in enumerate(crosses):
            at = h * size
            byte_ref[start : start + TILE, at : at + size] = (
                cross * scale * dgain_ref[:, at : at + size]
            ).astype(jnp.bfloat16)


def patches(at, blocks, weights, plan, n_copies, up_shape, kv_shape, encoded, bias, gains, starts_col, starts_row, n_patch_width):
    rows = sum(b.shape[0] for b in blocks)
    slots = starts_col.shape[0]
    return pl.pallas_call(
        functools.partial(patch_kernel, len(blocks), plan, len(weights)),
        in_specs=[pl.BlockSpec(memory_space=pltpu.SMEM)]
        + [VMEM] * len(blocks)
        + [ANY] * len(weights)
        + [VMEM] * 7,
        out_specs=[VMEM, VMEM],
        out_shape=[
            jax.ShapeDtypeStruct(encoded.shape, jnp.bfloat16),
            jax.ShapeDtypeStruct((slots, n_patch_width), jnp.bfloat16),
        ],
        scratch_shapes=[
            pltpu.VMEM(up_shape, jnp.bfloat16),
            pltpu.VMEM(kv_shape, jnp.bfloat16),
            pltpu.VMEM((rows, kv_shape[1]), jnp.bfloat16),
            pltpu.VMEM((slots, n_patch_width), jnp.float32),
            pltpu.VMEM((slots, n_patch_width), jnp.bfloat16),
            pltpu.SemaphoreType.DMA((n_copies,)),
        ],
        compiler_params=pltpu.CompilerParams(vmem_limit_bytes=48 * 2**20),
        name="patches",
    )(at, *blocks, *weights, encoded, bias, *gains, starts_col, starts_row)


def exchanged(value, axis, mask):
    return lax.ppermute(value, axis, [(i, i ^ mask) for i in range(lax.axis_size(axis))])


def passed_along(value, axis, steps):
    count = lax.axis_size(axis)
    return lax.ppermute(value, axis, [(i, i + steps) for i in range(count - steps)])


def whole_plan(at_ref, weights, up_ref, kv_ref):
    return [(weights[0], up_ref), (weights[1], kv_ref)]


def quarter_plan(at_ref, weights, up_ref, kv_ref):
    z, doc = at_ref[0] // 2, at_ref[1]
    up_rows, up_cols = up_ref.shape[0] // 4, up_ref.shape[1] // 4
    kv_rows, kv_cols = kv_ref.shape[0] // 8, kv_ref.shape[1] // 4
    copies = []
    for i, ref in enumerate(weights):
        block, part = i // 4, i % 4
        zb, q = z ^ block, doc ^ part
        cols = pl.ds(pl.multiple_of(q * up_cols, up_cols), up_cols)
        rows = pl.ds(pl.multiple_of(zb * up_rows, up_rows), up_rows)
        copies.append((ref.at[:up_rows, :], up_ref.at[rows, cols]))
        cols = pl.ds(pl.multiple_of(q * kv_cols, kv_cols), kv_cols)
        for y in range(2):
            rows = pl.ds(pl.multiple_of((2 * zb + y) * kv_rows, kv_rows), kv_rows)
            copies.append((ref.at[up_rows:, y * kv_cols : (y + 1) * kv_cols], kv_ref.at[rows, cols]))
    return copies


def quarter_weights(w_up, w_kv):
    doc = lax.axis_index("doc")
    y = lax.axis_index("seq") % 2
    up = lax.dynamic_slice_in_dim(w_up, doc * (w_up.shape[1] // 4), w_up.shape[1] // 4, 1)
    kv = lax.dynamic_slice_in_dim(w_kv, doc * (w_kv.shape[1] // 4), w_kv.shape[1] // 4, 1)
    n = up.shape[0]
    piece = jnp.concatenate([up, jnp.concatenate([kv[:n], kv[n:]], axis=1)], axis=0)
    other = exchanged(piece, "seq", 1)
    low, high = jnp.where(y == 0, piece, other), jnp.where(y == 0, other, piece)

    def unpacked(p):
        w = p.shape[1] // 2
        return jnp.concatenate([p[n:, :w], p[n:, w:]], axis=0)

    mine = jnp.concatenate(
        [low[:n], high[:n], jnp.concatenate([unpacked(low), unpacked(high)], axis=1)], axis=0
    )
    blocks = [mine] + [exchanged(mine, "seq", 2 * j) for j in range(1, 4)]
    out = []
    for block in blocks:
        across = exchanged(block, "doc", 2)
        out += [block, exchanged(block, "doc", 1), across, exchanged(across, "doc", 1)]
    return out


def per_device(
    byte_q, byte_k, byte_v, byte_gain, pool_query, w_up, patch_gain, w_kv, out_gain, dec_gain,
    patch_start,
):
    nbytes = byte_q.shape[0]
    slots = patch_start.shape[1]
    device = lax.axis_index("seq")
    doc = lax.axis_index("doc")
    n_seq, n_doc = lax.axis_size("seq"), lax.axis_size("doc")
    paired = n_seq == 8 and n_doc == 4

    k_tail = passed_along(byte_k, "seq", 1)
    v_tail = passed_along(byte_v, "seq", 1)
    if paired:
        weights = quarter_weights(w_up, w_kv)
        plan, n_copies = quarter_plan, 3 * len(weights)
    else:
        weights = [lax.all_gather(w, "seq", axis=0, tiled=True) for w in (w_up, w_kv)]
        plan, n_copies = whole_plan, 2

    own, lse = own_attention(byte_q, byte_k, byte_v)
    starts = lax.dynamic_index_in_dim(patch_start, device, 0, keepdims=False)
    ends = jnp.concatenate([starts[1:], jnp.full((1,), nbytes, jnp.int32)])
    row = lambda g: g.astype(jnp.float32)[None, :]
    encoded, pooled = cross_attention(
        (device == 0).astype(jnp.int32)[None], byte_q, k_tail, v_tail, own, lse, row(byte_gain),
        pool_query, starts[:, None], ends[:, None],
    )

    place = jnp.arange(slots, dtype=jnp.int32)
    own_allowed = (place[None, :] <= place[:, None]) & (starts < nbytes)[None, :]
    if paired:
        zs = [exchanged(pooled, "seq", 2 * j) for j in range(1, 4)]
        ys = [exchanged(b, "seq", 1) for b in [pooled] + zs]
        blocks = [pooled] + zs + ys
        order = jnp.stack([device ^ m for m in (2, 4, 6, 1, 3, 5, 7)])
    else:
        blocks = [pooled, lax.all_gather(pooled, "seq", axis=0, tiled=True)]
        order = jnp.arange(n_seq, dtype=jnp.int32)
    live = (patch_start < nbytes)[order] & (order < device)[:, None]
    allowed = jnp.concatenate(
        [own_allowed, jnp.broadcast_to(live.reshape(1, -1), (slots, live.size))], axis=1
    )
    bias = jnp.where(allowed, 0.0, LOW).astype(jnp.float32)
    at = jnp.stack([device, doc]).astype(jnp.int32)
    byte_out, patch_out = patches(
        at, blocks, weights, plan, n_copies,
        (w_up.shape[0] * n_seq, w_up.shape[1]), (w_kv.shape[0] * n_seq, w_kv.shape[1]),
        encoded, bias, [row(patch_gain), row(out_gain), row(dec_gain)],
        starts[:, None], starts[None, :], w_up.shape[1],
    )
    return (byte_out, patch_out)


def solution(mesh):
    placed = (
        P(("doc", "seq"), None),
        P(("doc", "seq"), None),
        P(("doc", "seq"), None),
        P(),
        P(),
        P("seq", None),
        P(),
        P("seq", None),
        P(),
        P(),
        P("doc", None),
    )
    return jax.shard_map(
        per_device,
        mesh=mesh,
        in_specs=placed,
        out_specs=(P(("doc", "seq"), None), P(("doc", "seq"), None)),
        check_vma=False,
    )
```

```python
import functools

import jax
import jax.numpy as jnp
from jax import lax
from jax.experimental import pallas as pl
from jax.experimental.pallas import tpu as pltpu
from jax.sharding import PartitionSpec as P

PATCH_QUERY_HEADS = 32
PATCH_KEY_HEADS = 8
LOG2E = 1.4426950408889634
LOW = -1e30
TILE = 128
epsilon = 1e-06
VMEM = pl.BlockSpec(memory_space=pltpu.VMEM)
SMALL = pl.CostEstimate(flops=1, bytes_accessed=1, transcendentals=0)
ANY = pl.BlockSpec(memory_space=pl.ANY)


def dot_t(a, b):
    return lax.dot_general(a, b, (((1,), (1,)), ((), ())), preferred_element_type=jnp.float32)


def dot(a, b):
    return jnp.dot(a, b, preferred_element_type=jnp.float32)


def split(value):
    high = value.astype(jnp.bfloat16)
    rest = value - high.astype(jnp.float32)
    middle = rest.astype(jnp.bfloat16)
    return high, middle, (rest - middle.astype(jnp.float32)).astype(jnp.bfloat16)


def keep_lse(ref, base, rows, head, lse):
    n = (ref.shape[0] - base) // 4
    across = jnp.transpose(lse)[: 4 * n, :]
    row = lax.broadcasted_iota(jnp.int32, across.shape, 0)
    kept = jnp.where(head == 0, 0.0, ref[base:, rows].astype(jnp.float32))
    for i, term in enumerate(split(across)):
        kept = jnp.where(row == head + i * n, term.astype(jnp.float32), kept)
    ref[base:, rows] = kept.astype(jnp.bfloat16)


def own_kernel(q_ref, k_ref, v_ref, mix_ref, lse_ref):
    head = pl.program_id(0)
    nbytes, size = q_ref.shape
    factor = size ** (-0.5) * LOG2E
    row = lax.broadcasted_iota(jnp.int32, (TILE, TILE), 0)
    col = lax.broadcasted_iota(jnp.int32, (TILE, TILE), 1)
    causal = col <= row
    values = jnp.concatenate([v_ref[...], jnp.ones((nbytes, size), jnp.bfloat16)], axis=1)

    for start in range(0, nbytes, TILE):
        end = start + TILE
        scores = dot_t(q_ref[start:end, :], k_ref[:end, :])
        last = jnp.where(causal, scores[:, start:end], LOW)
        scores = last if start == 0 else jnp.concatenate([scores[:, :start], last], axis=1)
        peak = jnp.max(scores, axis=1, keepdims=True)
        expo = jnp.exp2((scores - peak) * factor).astype(jnp.bfloat16)
        total = dot(expo, values[:end])
        mix_ref[start:end, :] = total[:, :size] / total[:, size:]
        keep_lse(lse_ref, 0, slice(start, end), head, peak * factor + jnp.log2(total[:, size:]))


def own_attention(q, k, v):
    nbytes, width = q.shape
    block = pl.BlockSpec((nbytes, TILE), lambda h: (0, h))
    return pl.pallas_call(
        own_kernel,
        grid=(width // TILE,),
        in_specs=[block] * 3,
        out_specs=[block, pl.BlockSpec((4 * (width // TILE), nbytes), lambda h: (0, 0))],
        out_shape=[
            jax.ShapeDtypeStruct((nbytes, width), jnp.float32),
            jax.ShapeDtypeStruct((4 * (width // TILE), nbytes), jnp.bfloat16),
        ],
        cost_estimate=SMALL,
        compiler_params=pltpu.CompilerParams(vmem_limit_bytes=24 * 2**20),
        name="own_attention",
    )(q, k, v)


def cross_kernel(q_ref, k_ref, v_ref, out_ref):
    head = pl.program_id(0)
    nbytes, size = q_ref.shape
    factor = size ** (-0.5) * LOG2E
    row = lax.broadcasted_iota(jnp.int32, (TILE, TILE), 0)
    col = lax.broadcasted_iota(jnp.int32, (TILE, TILE), 1)
    values = jnp.concatenate([v_ref[...], jnp.ones((nbytes, size), jnp.bfloat16)], axis=1)
    columns = pl.ds(pl.multiple_of(head * size, size), size)

    for start in range(0, nbytes, TILE):
        end = start + TILE
        scores = dot_t(q_ref[start:end, :], k_ref[start:, :])
        first = jnp.where(col > row, scores[:, :TILE], LOW)
        scores = jnp.concatenate([first, scores[:, TILE:]], axis=1) if end < nbytes else first
        peak = jnp.max(scores, axis=1, keepdims=True)
        expo = jnp.exp2((scores - peak) * factor)
        if end == nbytes:
            expo = jnp.where(col > row, expo, 0.0)
        total = dot(expo.astype(jnp.bfloat16), values[start:])
        norm = total[:, size:]
        some = norm > 0
        norm = jnp.where(some, norm, 1.0)
        out_ref[start:end, columns] = (total[:, :size] / norm).astype(jnp.bfloat16)
        lse = jnp.where(some, peak * factor + jnp.log2(norm), LOW)
        keep_lse(out_ref, nbytes, slice(start, end), head, lse)


def cross_attention(q, k, v, first, count):
    nbytes, width = q.shape
    block = pl.BlockSpec((nbytes, TILE), lambda h: (0, h + first))
    out = (nbytes + 4 * count, count * TILE)
    return pl.pallas_call(
        cross_kernel,
        grid=(count,),
        in_specs=[pl.BlockSpec((nbytes, TILE), lambda h: (0, h)), block, block],
        out_specs=pl.BlockSpec(out, lambda h: (0, 0)),
        out_shape=jax.ShapeDtypeStruct(out, jnp.bfloat16),
        cost_estimate=SMALL,
        compiler_params=pltpu.CompilerParams(vmem_limit_bytes=24 * 2**20),
        name="cross_attention",
    )(q, k, v)


def spread(terms, first, count):
    n = terms.shape[0] // 4
    row = lax.broadcasted_iota(jnp.int32, (4 * n, count * TILE), 0)
    col = lax.broadcasted_iota(jnp.int32, (4 * n, count * TILE), 1) // TILE + first
    one = jnp.where((row % n == col) & (row < 3 * n), 1.0, 0.0).astype(jnp.bfloat16)
    return lax.dot_general(terms, one, (((0,), (0,)), ((), ())), preferred_element_type=jnp.float32)


def pool_kernel(
    lead_ref, own_ref, lse_ref, *refs
):
    *part_refs, gain_ref, query_ref, start_ref, next_ref, enc_ref, pooled_ref = refs
    nbytes, width = own_ref.shape
    slots = start_ref.shape[0]
    size = TILE
    factor = size ** (-0.5) * LOG2E
    leading = lead_ref[0] != 0
    for start in range(0, nbytes, TILE):
        rows = slice(start, start + TILE)
        mixes = []
        squares = jnp.zeros((TILE, size), jnp.float32)
        first = 0
        for part_ref in part_refs:
            count = part_ref.shape[1] // TILE
            own_lse = spread(lse_ref[:, rows], first, count)
            part_lse = spread(part_ref[nbytes:, rows], 0, count)
            for h in range(count):
                at = slice(h * size, (h + 1) * size)
                gap = jnp.where(leading, LOW, part_lse[:, at] - own_lse[:, at])
                share = 1.0 / (1.0 + jnp.exp2(gap))
                own = own_ref[rows, (first + h) * size : (first + h + 1) * size]
                part = part_ref[rows, at].astype(jnp.float32)
                mix = part + (own - part) * share
                squares += mix * mix
                mixes.append(mix)
            first += count
        scale = lax.rsqrt(jnp.sum(squares, axis=1, keepdims=True) / width + epsilon)
        for h, mix in enumerate(mixes):
            at = slice(h * size, (h + 1) * size)
            enc_ref[rows, at] = (mix * scale * gain_ref[:, at]).astype(jnp.bfloat16)
    enc = enc_ref[...]
    n_heads = query_ref.shape[0]
    wide = jnp.concatenate([query_ref[...].astype(jnp.float32)] * n_heads, axis=1)
    head_row = lax.broadcasted_iota(jnp.int32, wide.shape, 0)
    head_col = lax.broadcasted_iota(jnp.int32, wide.shape, 1) // size
    wide = jnp.where(head_row == head_col, wide, 0.0).astype(jnp.bfloat16)
    scores = dot_t(wide, enc) * factor
    place = lax.broadcasted_iota(jnp.int32, (slots, nbytes), 1)
    member = (place >= start_ref[...]) & (place < next_ref[...])
    for h in range(n_heads):
        inside = jnp.where(member, scores[h : h + 1, :], LOW)
        peak = jnp.max(inside, axis=1, keepdims=True)
        expo = jnp.where(member, jnp.exp2(inside - peak), 0.0)
        total = jnp.sum(expo, axis=1, keepdims=True)
        weights = (expo * jnp.where(total > 0, 1.0 / total, 0.0)).astype(jnp.bfloat16)
        pooled_ref[:, h * size : (h + 1) * size] = dot(
            weights, enc[:, h * size : (h + 1) * size]
        ).astype(jnp.bfloat16)


def pool(leading, own, lse, parts, gain, pool_query, starts, ends):
    nbytes, width = own.shape
    slots = starts.shape[0]
    return pl.pallas_call(
        pool_kernel,
        in_specs=[pl.BlockSpec(memory_space=pltpu.SMEM)] + [VMEM] * (len(parts) + 6),
        out_specs=[VMEM, VMEM],
        out_shape=[
            jax.ShapeDtypeStruct((nbytes, width), jnp.bfloat16),
            jax.ShapeDtypeStruct((slots, width), jnp.bfloat16),
        ],
        cost_estimate=SMALL,
        compiler_params=pltpu.CompilerParams(vmem_limit_bytes=32 * 2**20),
        name="pool",
    )(leading, own, lse, *parts, gain, pool_query, starts, ends)


def patch_kernel(n_blocks, plan, n_weights, at_ref, *refs):
    blocks = refs[:n_blocks]
    weights = refs[n_blocks : n_blocks + n_weights]
    (
        enc_ref, bias_ref, pgain_ref, ogain_ref, dgain_ref, start_col_ref, start_row_ref,
        byte_ref, patch_ref, all_ref, up_ref, kv_w_ref, kv_ref, mix_ref, in_ref, sems,
    ) = refs[n_blocks + n_weights :]
    copies = plan(at_ref, weights, up_ref, kv_w_ref)
    copies = [
        pltpu.make_async_copy(source, target, sems.at[i]) for i, (source, target) in enumerate(copies)
    ]
    for copy in copies:
        copy.start()
    for copy in copies:
        copy.wait()

    slots = patch_ref.shape[0]
    offset = 0
    for block in blocks:
        all_ref[offset : offset + block.shape[0], :] = block[...]
        offset += block.shape[0]
    step = 4 * slots
    for r in range(0, offset, step):
        rows = slice(r, min(r + step, offset))
        lifted = dot(all_ref[rows, :], up_ref[...])
        scale = lax.rsqrt(jnp.mean(lifted * lifted, axis=1, keepdims=True) + epsilon)
        patch_in = (lifted * scale * pgain_ref[...]).astype(jnp.bfloat16)
        if r == 0:
            in_ref[...] = patch_in[:slots]
        kv_ref[rows, :] = dot(patch_in, kv_w_ref[...]).astype(jnp.bfloat16)

    size = patch_ref.shape[1] // PATCH_QUERY_HEADS
    rows = kv_ref.shape[0]
    half_width = PATCH_KEY_HEADS * size
    factor = size ** (-0.5) * LOG2E
    groups = PATCH_QUERY_HEADS // PATCH_KEY_HEADS
    pair = 2 * size
    lane_half = lax.broadcasted_iota(jnp.int32, (slots, pair), 1) // size
    ones = jnp.ones((rows, pair), jnp.bfloat16)
    for kp in range(PATCH_KEY_HEADS // 2):
        keys = kv_ref[:, kp * pair : (kp + 1) * pair]
        values = jnp.concatenate(
            [kv_ref[:, half_width + kp * pair : half_width + (kp + 1) * pair], ones], axis=1
        )
        for half in range(2):
            first = (2 * kp + half) * groups
            queries = []
            for g in range(groups):
                at = (first + g) // 2 * pair
                q = in_ref[:, at : at + pair].astype(jnp.float32)
                if g % 2 != half:
                    q = pltpu.roll(q, size, 1)
                queries.append(jnp.where(lane_half == half, q, 0.0).astype(jnp.bfloat16))
            scores = dot_t(jnp.concatenate(queries, axis=0), keys)
            outs = []
            for g in range(groups):
                part = scores[g * slots : (g + 1) * slots, :] * factor + bias_ref[...]
                peak = jnp.max(part, axis=1, keepdims=True)
                outs.append(jnp.exp2(part - peak).astype(jnp.bfloat16))
            total = dot(jnp.concatenate(outs, axis=0), values)
            mixed = total[:, :pair] / total[:, pair:]
            for g in range(0, groups, 2):
                two = [mixed[(g + i) * slots : (g + i + 1) * slots, :] for i in range(2)]
                two = [t if i == half else pltpu.roll(t, size, 1) for i, t in enumerate(two)]
                at = (first + g) // 2 * pair
                mix_ref[:, at : at + pair] = jnp.where(lane_half == 0, two[0], two[1])

    nbytes = enc_ref.shape[0]
    mix = mix_ref[...]
    scale = lax.rsqrt(jnp.mean(mix * mix, axis=1, keepdims=True) + epsilon)
    alive = jnp.where(start_col_ref[...] < nbytes, 1.0, 0.0)
    patch_ref[...] = (mix * scale * ogain_ref[...] * alive).astype(jnp.bfloat16)

    width = enc_ref.shape[1]
    size = TILE
    factor = size ** (-0.5) * LOG2E
    ones = jnp.ones((slots, size), jnp.bfloat16)
    for start in range(0, nbytes, TILE):
        place = lax.broadcasted_iota(jnp.int32, (TILE, slots), 0) + start
        allowed = start_row_ref[...] <= place
        crosses = []
        squares = jnp.zeros((TILE, size), jnp.float32)
        for h in range(width // size):
            scores = dot_t(
                enc_ref[start : start + TILE, h * size : (h + 1) * size],
                patch_ref[:, 2 * h * size : (2 * h + 1) * size],
            )
            scores = jnp.where(allowed, scores * factor, LOW)
            peak = jnp.max(scores, axis=1, keepdims=True)
            expo = jnp.exp2(scores - peak).astype(jnp.bfloat16)
            values = jnp.concatenate(
                [patch_ref[:, (2 * h + 1) * size : (2 * h + 2) * size], ones], axis=1
            )
            total = dot(expo, values)
            cross = total[:, :size] / total[:, size:]
            squares += cross * cross
            crosses.append(cross)
        scale = lax.rsqrt(jnp.sum(squares, axis=1, keepdims=True) / width + epsilon)
        for h, cross in enumerate(crosses):
            at = h * size
            byte_ref[start : start + TILE, at : at + size] = (
                cross * scale * dgain_ref[:, at : at + size]
            ).astype(jnp.bfloat16)


def patches(at, blocks, weights, plan, n_copies, up_shape, kv_shape, encoded, bias, gains, starts_col, starts_row, n_patch_width):
    rows = sum(b.shape[0] for b in blocks)
    slots = starts_col.shape[0]
    return pl.pallas_call(
        functools.partial(patch_kernel, len(blocks), plan, len(weights)),
        in_specs=[pl.BlockSpec(memory_space=pltpu.SMEM)]
        + [VMEM] * len(blocks)
        + [ANY] * len(weights)
        + [VMEM] * 7,
        out_specs=[VMEM, VMEM],
        out_shape=[
            jax.ShapeDtypeStruct(encoded.shape, jnp.bfloat16),
            jax.ShapeDtypeStruct((slots, n_patch_width), jnp.bfloat16),
        ],
        scratch_shapes=[
            pltpu.VMEM((rows, up_shape[0]), jnp.bfloat16),
            pltpu.VMEM(up_shape, jnp.bfloat16),
            pltpu.VMEM(kv_shape, jnp.bfloat16),
            pltpu.VMEM((rows, kv_shape[1]), jnp.bfloat16),
            pltpu.VMEM((slots, n_patch_width), jnp.float32),
            pltpu.VMEM((slots, n_patch_width), jnp.bfloat16),
            pltpu.SemaphoreType.DMA((n_copies,)),
        ],
        cost_estimate=SMALL,
        compiler_params=pltpu.CompilerParams(vmem_limit_bytes=48 * 2**20),
        name="patches",
    )(at, *blocks, *weights, encoded, bias, *gains, starts_col, starts_row)


def exchanged(value, axis, mask):
    return lax.ppermute(value, axis, [(i, i ^ mask) for i in range(lax.axis_size(axis))])


def passed_along(value, axis, steps):
    count = lax.axis_size(axis)
    pairs = [(i, i + steps) for i in range(count) if 0 <= i + steps < count]
    return lax.ppermute(value, axis, pairs)


def whole_plan(at_ref, weights, up_ref, kv_ref):
    return [(weights[0], up_ref), (weights[1], kv_ref)]


def quarter_plan(at_ref, weights, up_ref, kv_ref):
    z, doc = at_ref[0] // 2, at_ref[1]
    up_rows, up_cols = up_ref.shape[0] // 4, up_ref.shape[1] // 4
    kv_rows, kv_cols = kv_ref.shape[0] // 8, kv_ref.shape[1] // 4
    copies = []
    for i, ref in enumerate(weights):
        block, part = i // 4, i % 4
        zb, q = z ^ block, doc ^ part
        cols = pl.ds(pl.multiple_of(q * up_cols, up_cols), up_cols)
        rows = pl.ds(pl.multiple_of(zb * up_rows, up_rows), up_rows)
        copies.append((ref.at[:up_rows, :], up_ref.at[rows, cols]))
        cols = pl.ds(pl.multiple_of(q * kv_cols, kv_cols), kv_cols)
        for y in range(2):
            rows = pl.ds(pl.multiple_of((2 * zb + y) * kv_rows, kv_rows), kv_rows)
            copies.append((ref.at[up_rows:, y * kv_cols : (y + 1) * kv_cols], kv_ref.at[rows, cols]))
    return copies


def paired_weights(w_up, w_kv):
    doc = lax.axis_index("doc")
    y = lax.axis_index("seq") % 2
    up = lax.dynamic_slice_in_dim(w_up, doc * (w_up.shape[1] // 4), w_up.shape[1] // 4, 1)
    kv = lax.dynamic_slice_in_dim(w_kv, doc * (w_kv.shape[1] // 4), w_kv.shape[1] // 4, 1)
    n = up.shape[0]
    piece = jnp.concatenate([up, jnp.concatenate([kv[:n], kv[n:]], axis=1)], axis=0)
    other = exchanged(piece, "seq", 1)
    low, high = jnp.where(y == 0, piece, other), jnp.where(y == 0, other, piece)

    def unpacked(p):
        w = p.shape[1] // 2
        return jnp.concatenate([p[n:, :w], p[n:, w:]], axis=0)

    mine = jnp.concatenate(
        [low[:n], high[:n], jnp.concatenate([unpacked(low), unpacked(high)], axis=1)], axis=0
    )
    return mine, other


def after(value, *others):
    return lax.optimization_barrier((value,) + others)[0]


def per_device(
    byte_q, byte_k, byte_v, byte_gain, pool_query, w_up, patch_gain, w_kv, out_gain, dec_gain,
    patch_start,
):
    nbytes = byte_q.shape[0]
    slots = patch_start.shape[1]
    device = lax.axis_index("seq")
    doc = lax.axis_index("doc")
    n_seq, n_doc = lax.axis_size("seq"), lax.axis_size("doc")
    paired = n_seq == 8 and n_doc == 4

    count = byte_q.shape[1] // TILE // 2
    halves = [byte_q[:, i * count * TILE : (i + 1) * count * TILE] for i in range(2)]
    if paired:
        mine, other = paired_weights(w_up, w_kv)
        halves = [after(h, other) for h in halves]
        byte_q = after(byte_q, other)
    q_next = [passed_along(h, "seq", -1) for h in halves]
    if paired:
        z_blocks = [exchanged(mine, "seq", 2 * j) for j in (1, 2)]
        z_blocks.append(exchanged(after(mine, q_next[0]), "seq", 6))
        across = [exchanged(mine, "doc", 2)]
    own, lse = own_attention(byte_q, byte_k, byte_v)
    first = [lse] + (across[:1] if paired else [])
    low = cross_attention(after(q_next[0], *first), byte_k, byte_v, 0, count)
    second = [low] + (z_blocks[:1] if paired else [])
    high = cross_attention(after(q_next[1], *second), byte_k, byte_v, count, count)
    parts = [passed_along(partial, "seq", 1) for partial in (low, high)]
    if paired:
        across += [exchanged(after(z, high), "doc", 2) for z in z_blocks[:2]]
        parts[1] = after(parts[1], z_blocks[1], z_blocks[2], across[1])

    starts = lax.dynamic_index_in_dim(patch_start, device, 0, keepdims=False)
    ends = jnp.concatenate([starts[1:], jnp.full((1,), nbytes, jnp.int32)])
    row = lambda g: g.astype(jnp.float32)[None, :]
    encoded, pooled = pool(
        (device == 0).astype(jnp.int32)[None], own, lse, parts, row(byte_gain), pool_query,
        starts[:, None], ends[:, None],
    )
    if paired:
        across.append(exchanged(after(z_blocks[2], pooled), "doc", 2))
        weights = []
        for z, x in zip([mine] + z_blocks, across):
            weights += [z, exchanged(after(z, pooled), "doc", 1), x, exchanged(after(x, pooled), "doc", 1)]
        plan, n_copies = quarter_plan, 3 * len(weights)
    else:
        weights = [lax.all_gather(w, "seq", axis=0, tiled=True) for w in (w_up, w_kv)]
        plan, n_copies = whole_plan, 2

    place = jnp.arange(slots, dtype=jnp.int32)
    own_allowed = (place[None, :] <= place[:, None]) & (starts < nbytes)[None, :]
    if paired:
        zs = [exchanged(pooled, "seq", 2 * j) for j in range(1, 4)]
        ys = [exchanged(b, "seq", 1) for b in [pooled] + zs]
        blocks = [pooled] + zs + ys
        order = jnp.stack([device ^ m for m in (2, 4, 6, 1, 3, 5, 7)])
    else:
        blocks = [pooled, lax.all_gather(pooled, "seq", axis=0, tiled=True)]
        order = jnp.arange(n_seq, dtype=jnp.int32)
    live = (patch_start < nbytes)[order] & (order < device)[:, None]
    allowed = jnp.concatenate(
        [own_allowed, jnp.broadcast_to(live.reshape(1, -1), (slots, live.size))], axis=1
    )
    bias = jnp.where(allowed, 0.0, LOW).astype(jnp.float32)
    at = jnp.stack([device, doc]).astype(jnp.int32)
    byte_out, patch_out = patches(
        at, blocks, weights, plan, n_copies,
        (w_up.shape[0] * n_seq, w_up.shape[1]), (w_kv.shape[0] * n_seq, w_kv.shape[1]),
        encoded, bias, [row(patch_gain), row(out_gain), row(dec_gain)],
        starts[:, None], starts[None, :], w_up.shape[1],
    )
    return (byte_out, patch_out)


def solution(mesh):
    placed = (
        P(("doc", "seq"), None),
        P(("doc", "seq"), None),
        P(("doc", "seq"), None),
        P(),
        P(),
        P("seq", None),
        P(),
        P("seq", None),
        P(),
        P(),
        P("doc", None),
    )
    return jax.shard_map(
        per_device,
        mesh=mesh,
        in_specs=placed,
        out_specs=(P(("doc", "seq"), None), P(("doc", "seq"), None)),
        check_vma=False,
    )
```

```python
import functools

import jax
import jax.numpy as jnp
from jax import lax
from jax.experimental import pallas as pl
from jax.experimental.pallas import tpu as pltpu
from jax.sharding import PartitionSpec as P

PATCH_QUERY_HEADS = 32
PATCH_KEY_HEADS = 8
LOG2E = 1.4426950408889634
LOW = -1e30
TILE = 128
GROUP = 4
epsilon = 1e-06
VMEM = pl.BlockSpec(memory_space=pltpu.VMEM)
SMALL = pl.CostEstimate(flops=1, bytes_accessed=1, transcendentals=0)
ANY = pl.BlockSpec(memory_space=pl.ANY)


def dot_t(a, b):
    return lax.dot_general(a, b, (((1,), (1,)), ((), ())), preferred_element_type=jnp.float32)


def dot(a, b):
    return jnp.dot(a, b, preferred_element_type=jnp.float32)


def split(value):
    high = value.astype(jnp.bfloat16)
    rest = value - high.astype(jnp.float32)
    middle = rest.astype(jnp.bfloat16)
    return high, middle, (rest - middle.astype(jnp.float32)).astype(jnp.bfloat16)


def keep_lse(ref, base, columns_ref, count):
    for start in range(0, columns_ref.shape[0], TILE):
        rows = slice(start, start + TILE)
        across = jnp.transpose(columns_ref[rows, :])[:count, :]
        terms = [term.astype(jnp.float32) for term in split(across)]
        terms.append(jnp.zeros_like(across))
        ref[base:, rows] = jnp.concatenate(terms, axis=0).astype(jnp.bfloat16)


def own_kernel(q_ref, k_ref, v_ref, mix_ref, lse_ref, columns_ref):
    step = pl.program_id(0)
    nbytes, width = q_ref.shape
    size = TILE
    factor = size ** (-0.5) * LOG2E
    row = lax.broadcasted_iota(jnp.int32, (TILE, TILE), 0)
    col = lax.broadcasted_iota(jnp.int32, (TILE, TILE), 1)
    causal = col <= row
    ones = jnp.ones((nbytes, size), jnp.bfloat16)

    for h in range(width // size):
        at = slice(h * size, (h + 1) * size)
        values = jnp.concatenate([v_ref[:, at], ones], axis=1)
        head = step * (width // size) + h
        for start in range(0, nbytes, TILE):
            end = start + TILE
            scores = dot_t(q_ref[start:end, at], k_ref[:end, at])
            last = jnp.where(causal, scores[:, start:end], LOW)
            scores = last if start == 0 else jnp.concatenate([scores[:, :start], last], axis=1)
            peak = jnp.max(scores, axis=1, keepdims=True)
            expo = jnp.exp2((scores - peak) * factor).astype(jnp.bfloat16)
            total = dot(expo, values[:end])
            mix_ref[start:end, at] = (total[:, :size] / total[:, size:]).astype(jnp.bfloat16)
            lse = peak * factor + jnp.log2(total[:, size:])
            columns_ref[start:end, :] = jnp.where(col == head, lse, columns_ref[start:end, :])

    @pl.when(step == pl.num_programs(0) - 1)
    def _():
        keep_lse(lse_ref, 0, columns_ref, lse_ref.shape[0] // 4)


def own_attention(q, k, v):
    nbytes, width = q.shape
    block = pl.BlockSpec((nbytes, GROUP * TILE), lambda h: (0, h))
    rows = (4 * (width // TILE), nbytes)
    return pl.pallas_call(
        functools.partial(own_kernel),
        grid=(width // TILE // GROUP,),
        in_specs=[block] * 3,
        out_specs=[block, pl.BlockSpec(rows, lambda h: (0, 0))],
        out_shape=[
            jax.ShapeDtypeStruct((nbytes, width), jnp.bfloat16),
            jax.ShapeDtypeStruct(rows, jnp.bfloat16),
        ],
        scratch_shapes=[pltpu.VMEM((nbytes, TILE), jnp.float32)],
        cost_estimate=SMALL,
        compiler_params=pltpu.CompilerParams(vmem_limit_bytes=24 * 2**20),
        name="own_attention",
    )(q, k, v)


def cross_kernel(steps, q_ref, k_ref, v_ref, out_ref, columns_ref):
    step = pl.program_id(0)
    nbytes, width = q_ref.shape
    size = TILE
    factor = size ** (-0.5) * LOG2E
    row = lax.broadcasted_iota(jnp.int32, (TILE, TILE), 0)
    col = lax.broadcasted_iota(jnp.int32, (TILE, TILE), 1)
    ones = jnp.ones((nbytes, size), jnp.bfloat16)

    for h in range(width // size):
        at = slice(h * size, (h + 1) * size)
        values = jnp.concatenate([v_ref[:, at], ones], axis=1)
        head = step * (width // size) + h
        columns = pl.ds(pl.multiple_of(head * size, size), size)
        for start in range(0, nbytes, TILE):
            end = start + TILE
            scores = dot_t(q_ref[start:end, at], k_ref[start:, at])
            first = jnp.where(col > row, scores[:, :TILE], LOW)
            scores = jnp.concatenate([first, scores[:, TILE:]], axis=1) if end < nbytes else first
            peak = jnp.max(scores, axis=1, keepdims=True)
            expo = jnp.exp2((scores - peak) * factor)
            if end == nbytes:
                expo = jnp.where(col > row, expo, 0.0)
            total = dot(expo.astype(jnp.bfloat16), values[start:])
            norm = total[:, size:]
            some = norm > 0
            norm = jnp.where(some, norm, 1.0)
            out_ref[start:end, columns] = (total[:, :size] / norm).astype(jnp.bfloat16)
            lse = jnp.where(some, peak * factor + jnp.log2(norm), LOW)
            columns_ref[start:end, :] = jnp.where(col == head, lse, columns_ref[start:end, :])

    @pl.when(step == steps - 1)
    def _():
        keep_lse(out_ref, nbytes, columns_ref, steps * (width // size))


def cross_attention(q, k, v, first, count):
    nbytes, width = q.shape
    size = GROUP * TILE
    block = pl.BlockSpec((nbytes, size), lambda h: (0, h + first // GROUP))
    out = (nbytes + 4 * count, count * TILE)
    return pl.pallas_call(
        functools.partial(cross_kernel, count // GROUP),
        grid=(count // GROUP,),
        in_specs=[pl.BlockSpec((nbytes, size), lambda h: (0, h)), block, block],
        out_specs=pl.BlockSpec(out, lambda h: (0, 0)),
        out_shape=jax.ShapeDtypeStruct(out, jnp.bfloat16),
        scratch_shapes=[pltpu.VMEM((nbytes, TILE), jnp.float32)],
        cost_estimate=SMALL,
        compiler_params=pltpu.CompilerParams(vmem_limit_bytes=24 * 2**20),
        name="cross_attention",
    )(q, k, v)


def spread(terms, first, count):
    n = terms.shape[0] // 4
    row = lax.broadcasted_iota(jnp.int32, (4 * n, count * TILE), 0)
    col = lax.broadcasted_iota(jnp.int32, (4 * n, count * TILE), 1) // TILE + first
    one = jnp.where((row % n == col) & (row < 3 * n), 1.0, 0.0).astype(jnp.bfloat16)
    return lax.dot_general(terms, one, (((0,), (0,)), ((), ())), preferred_element_type=jnp.float32)


def pool_kernel(
    lead_ref, own_ref, lse_ref, *refs
):
    *part_refs, gain_ref, query_ref, start_ref, next_ref, enc_ref, pooled_ref = refs
    nbytes, width = own_ref.shape
    slots = start_ref.shape[0]
    size = TILE
    factor = size ** (-0.5) * LOG2E
    leading = lead_ref[0] != 0
    for start in range(0, nbytes, TILE):
        rows = slice(start, start + TILE)
        mixes = []
        squares = jnp.zeros((TILE, size), jnp.float32)
        first = 0
        for part_ref in part_refs:
            count = part_ref.shape[1] // TILE
            own_lse = spread(lse_ref[:, rows], first, count)
            part_lse = spread(part_ref[nbytes:, rows], 0, count)
            for h in range(count):
                at = slice(h * size, (h + 1) * size)
                gap = jnp.where(leading, LOW, part_lse[:, at] - own_lse[:, at])
                share = 1.0 / (1.0 + jnp.exp2(gap))
                own = own_ref[rows, (first + h) * size : (first + h + 1) * size].astype(jnp.float32)
                part = part_ref[rows, at].astype(jnp.float32)
                mix = part + (own - part) * share
                squares += mix * mix
                mixes.append(mix)
            first += count
        scale = lax.rsqrt(jnp.sum(squares, axis=1, keepdims=True) / width + epsilon)
        for h, mix in enumerate(mixes):
            at = slice(h * size, (h + 1) * size)
            enc_ref[rows, at] = (mix * scale * gain_ref[:, at]).astype(jnp.bfloat16)
    enc = enc_ref[...]
    n_heads = query_ref.shape[0]
    wide = jnp.concatenate([query_ref[...].astype(jnp.float32)] * n_heads, axis=1)
    head_row = lax.broadcasted_iota(jnp.int32, wide.shape, 0)
    head_col = lax.broadcasted_iota(jnp.int32, wide.shape, 1) // size
    wide = jnp.where(head_row == head_col, wide, 0.0).astype(jnp.bfloat16)
    scores = dot_t(wide, enc) * factor
    place = lax.broadcasted_iota(jnp.int32, (slots, nbytes), 1)
    member = (place >= start_ref[...]) & (place < next_ref[...])
    for h in range(n_heads):
        inside = jnp.where(member, scores[h : h + 1, :], LOW)
        peak = jnp.max(inside, axis=1, keepdims=True)
        expo = jnp.where(member, jnp.exp2(inside - peak), 0.0)
        total = jnp.sum(expo, axis=1, keepdims=True)
        weights = (expo * jnp.where(total > 0, 1.0 / total, 0.0)).astype(jnp.bfloat16)
        pooled_ref[:, h * size : (h + 1) * size] = dot(
            weights, enc[:, h * size : (h + 1) * size]
        ).astype(jnp.bfloat16)


def pool(leading, own, lse, parts, gain, pool_query, starts, ends):
    nbytes, width = own.shape
    slots = starts.shape[0]
    return pl.pallas_call(
        pool_kernel,
        in_specs=[pl.BlockSpec(memory_space=pltpu.SMEM)] + [VMEM] * (len(parts) + 6),
        out_specs=[VMEM, VMEM],
        out_shape=[
            jax.ShapeDtypeStruct((nbytes, width), jnp.bfloat16),
            jax.ShapeDtypeStruct((slots, width), jnp.bfloat16),
        ],
        cost_estimate=SMALL,
        compiler_params=pltpu.CompilerParams(vmem_limit_bytes=32 * 2**20),
        name="pool",
    )(leading, own, lse, *parts, gain, pool_query, starts, ends)


def patch_kernel(n_blocks, plan, n_weights, at_ref, *refs):
    blocks = refs[:n_blocks]
    weights = refs[n_blocks : n_blocks + n_weights]
    (
        enc_ref, bias_ref, pgain_ref, ogain_ref, dgain_ref, start_col_ref, start_row_ref,
        byte_ref, patch_ref, all_ref, up_ref, kv_w_ref, kv_ref, mix_ref, in_ref, sems,
    ) = refs[n_blocks + n_weights :]
    ups, kvs = plan(at_ref, weights, up_ref, kv_w_ref)
    ups = [pltpu.make_async_copy(*copy, sems.at[i]) for i, copy in enumerate(ups)]
    kvs = [pltpu.make_async_copy(*copy, sems.at[len(ups) + i]) for i, copy in enumerate(kvs)]
    for copy in ups:
        copy.start()

    slots = patch_ref.shape[0]
    offset = 0
    for block in blocks:
        all_ref[offset : offset + block.shape[0], :] = block[...]
        offset += block.shape[0]
    step = 4 * slots
    for copy in ups:
        copy.wait()
    for copy in kvs:
        copy.start()
    for r in range(0, offset, step):
        rows = slice(r, min(r + step, offset))
        lifted = dot(all_ref[rows, :], up_ref[...])
        scale = lax.rsqrt(jnp.mean(lifted * lifted, axis=1, keepdims=True) + epsilon)
        in_ref[rows, :] = (lifted * scale * pgain_ref[...]).astype(jnp.bfloat16)
    for copy in kvs:
        copy.wait()
    for r in range(0, offset, step):
        rows = slice(r, min(r + step, offset))
        kv_ref[rows, :] = dot(in_ref[rows, :], kv_w_ref[...]).astype(jnp.bfloat16)

    size = patch_ref.shape[1] // PATCH_QUERY_HEADS
    rows = kv_ref.shape[0]
    half_width = PATCH_KEY_HEADS * size
    factor = size ** (-0.5) * LOG2E
    groups = PATCH_QUERY_HEADS // PATCH_KEY_HEADS
    pair = 2 * size
    lane_half = lax.broadcasted_iota(jnp.int32, (slots, pair), 1) // size
    ones = jnp.ones((rows, pair), jnp.bfloat16)
    for kp in range(PATCH_KEY_HEADS // 2):
        keys = kv_ref[:, kp * pair : (kp + 1) * pair]
        values = jnp.concatenate(
            [kv_ref[:, half_width + kp * pair : half_width + (kp + 1) * pair], ones], axis=1
        )
        for half in range(2):
            first = (2 * kp + half) * groups
            queries = []
            for g in range(groups):
                at = (first + g) // 2 * pair
                q = in_ref[:slots, at : at + pair].astype(jnp.float32)
                if g % 2 != half:
                    q = pltpu.roll(q, size, 1)
                queries.append(jnp.where(lane_half == half, q, 0.0).astype(jnp.bfloat16))
            scores = dot_t(jnp.concatenate(queries, axis=0), keys)
            outs = []
            for g in range(groups):
                part = scores[g * slots : (g + 1) * slots, :] * factor + bias_ref[...]
                peak = jnp.max(part, axis=1, keepdims=True)
                outs.append(jnp.exp2(part - peak).astype(jnp.bfloat16))
            total = dot(jnp.concatenate(outs, axis=0), values)
            mixed = total[:, :pair] / total[:, pair:]
            for g in range(0, groups, 2):
                two = [mixed[(g + i) * slots : (g + i + 1) * slots, :] for i in range(2)]
                two = [t if i == half else pltpu.roll(t, size, 1) for i, t in enumerate(two)]
                at = (first + g) // 2 * pair
                mix_ref[:, at : at + pair] = jnp.where(lane_half == 0, two[0], two[1])

    nbytes = enc_ref.shape[0]
    mix = mix_ref[...]
    scale = lax.rsqrt(jnp.mean(mix * mix, axis=1, keepdims=True) + epsilon)
    alive = jnp.where(start_col_ref[...] < nbytes, 1.0, 0.0)
    patch_ref[...] = (mix * scale * ogain_ref[...] * alive).astype(jnp.bfloat16)

    width = enc_ref.shape[1]
    size = TILE
    factor = size ** (-0.5) * LOG2E
    ones = jnp.ones((slots, size), jnp.bfloat16)
    for start in range(0, nbytes, 512):
        place = lax.broadcasted_iota(jnp.int32, (512, slots), 0) + start
        allowed = start_row_ref[...] <= place
        crosses = []
        squares = jnp.zeros((512, size), jnp.float32)
        for h in range(width // size):
            scores = dot_t(
                enc_ref[start : start + 512, h * size : (h + 1) * size],
                patch_ref[:, 2 * h * size : (2 * h + 1) * size],
            )
            scores = jnp.where(allowed, scores * factor, LOW)
            peak = jnp.max(scores, axis=1, keepdims=True)
            expo = jnp.exp2(scores - peak).astype(jnp.bfloat16)
            values = jnp.concatenate(
                [patch_ref[:, (2 * h + 1) * size : (2 * h + 2) * size], ones], axis=1
            )
            total = dot(expo, values)
            cross = total[:, :size] / total[:, size:]
            squares += cross * cross
            crosses.append(cross)
        scale = lax.rsqrt(jnp.sum(squares, axis=1, keepdims=True) / width + epsilon)
        for h, cross in enumerate(crosses):
            at = h * size
            byte_ref[start : start + 512, at : at + size] = (
                cross * scale * dgain_ref[:, at : at + size]
            ).astype(jnp.bfloat16)


def patches(at, blocks, weights, plan, n_copies, up_shape, kv_shape, encoded, bias, gains, starts_col, starts_row, n_patch_width):
    rows = sum(b.shape[0] for b in blocks)
    slots = starts_col.shape[0]
    return pl.pallas_call(
        functools.partial(patch_kernel, len(blocks), plan, len(weights)),
        in_specs=[pl.BlockSpec(memory_space=pltpu.SMEM)]
        + [VMEM] * len(blocks)
        + [ANY] * len(weights)
        + [VMEM] * 7,
        out_specs=[VMEM, VMEM],
        out_shape=[
            jax.ShapeDtypeStruct(encoded.shape, jnp.bfloat16),
            jax.ShapeDtypeStruct((slots, n_patch_width), jnp.bfloat16),
        ],
        scratch_shapes=[
            pltpu.VMEM((rows, up_shape[0]), jnp.bfloat16),
            pltpu.VMEM(up_shape, jnp.bfloat16),
            pltpu.VMEM(kv_shape, jnp.bfloat16),
            pltpu.VMEM((rows, kv_shape[1]), jnp.bfloat16),
            pltpu.VMEM((slots, n_patch_width), jnp.float32),
            pltpu.VMEM((rows, n_patch_width), jnp.bfloat16),
            pltpu.SemaphoreType.DMA((n_copies,)),
        ],
        cost_estimate=SMALL,
        compiler_params=pltpu.CompilerParams(vmem_limit_bytes=48 * 2**20),
        name="patches",
    )(at, *blocks, *weights, encoded, bias, *gains, starts_col, starts_row)


def exchanged(value, axis, mask):
    return lax.ppermute(value, axis, [(i, i ^ mask) for i in range(lax.axis_size(axis))])


def passed_along(value, axis, steps):
    count = lax.axis_size(axis)
    pairs = [(i, i + steps) for i in range(count) if 0 <= i + steps < count]
    return lax.ppermute(value, axis, pairs)


def whole_plan(at_ref, weights, up_ref, kv_ref):
    return [(weights[0], up_ref)], [(weights[1], kv_ref)]


def quarter_plan(at_ref, weights, up_ref, kv_ref):
    z, doc = at_ref[0] // 2, at_ref[1]
    up_rows, up_cols = up_ref.shape[0] // 4, up_ref.shape[1] // 4
    kv_rows, kv_cols = kv_ref.shape[0] // 8, kv_ref.shape[1] // 4
    ups, kvs = [], []
    for i, ref in enumerate(weights):
        block, part = i // 4, i % 4
        zb, q = z ^ block, doc ^ part
        cols = pl.ds(pl.multiple_of(q * up_cols, up_cols), up_cols)
        rows = pl.ds(pl.multiple_of(zb * up_rows, up_rows), up_rows)
        ups.append((ref.at[:up_rows, :], up_ref.at[rows, cols]))
        cols = pl.ds(pl.multiple_of(q * kv_cols, kv_cols), kv_cols)
        for y in range(2):
            rows = pl.ds(pl.multiple_of((2 * zb + y) * kv_rows, kv_rows), kv_rows)
            kvs.append((ref.at[up_rows:, y * kv_cols : (y + 1) * kv_cols], kv_ref.at[rows, cols]))
    return ups, kvs


def paired_weights(w_up, w_kv):
    doc = lax.axis_index("doc")
    y = lax.axis_index("seq") % 2
    up = lax.dynamic_slice_in_dim(w_up, doc * (w_up.shape[1] // 4), w_up.shape[1] // 4, 1)
    kv = lax.dynamic_slice_in_dim(w_kv, doc * (w_kv.shape[1] // 4), w_kv.shape[1] // 4, 1)
    n = up.shape[0]
    piece = jnp.concatenate([up, jnp.concatenate([kv[:n], kv[n:]], axis=1)], axis=0)
    other = exchanged(piece, "seq", 1)
    low, high = jnp.where(y == 0, piece, other), jnp.where(y == 0, other, piece)

    def unpacked(p):
        w = p.shape[1] // 2
        return jnp.concatenate([p[n:, :w], p[n:, w:]], axis=0)

    mine = jnp.concatenate(
        [low[:n], high[:n], jnp.concatenate([unpacked(low), unpacked(high)], axis=1)], axis=0
    )
    return mine, other


def after(value, *others):
    return lax.optimization_barrier((value,) + others)[0]


def per_device(
    byte_q, byte_k, byte_v, byte_gain, pool_query, w_up, patch_gain, w_kv, out_gain, dec_gain,
    patch_start,
):
    nbytes = byte_q.shape[0]
    slots = patch_start.shape[1]
    device = lax.axis_index("seq")
    doc = lax.axis_index("doc")
    n_seq, n_doc = lax.axis_size("seq"), lax.axis_size("doc")
    paired = n_seq == 8 and n_doc == 4

    count = byte_q.shape[1] // TILE // 2
    halves = [byte_q[:, i * count * TILE : (i + 1) * count * TILE] for i in range(2)]
    if paired:
        mine, other = paired_weights(w_up, w_kv)
        halves = [after(h, other) for h in halves]
        byte_q = after(byte_q, other)
    q_next = [passed_along(h, "seq", -1) for h in halves]
    if paired:
        z_blocks = [exchanged(mine, "seq", 2 * j) for j in (1, 2)]
        z_blocks.append(exchanged(z_blocks[1], "seq", 2))
        across = [exchanged(mine, "doc", 2)]
    own, lse = own_attention(byte_q, byte_k, byte_v)
    first = [lse] + (across[:1] if paired else [])
    low = cross_attention(after(q_next[0], *first), byte_k, byte_v, 0, count)
    second = [low]
    high = cross_attention(after(q_next[1], *second), byte_k, byte_v, count, count)
    parts = [passed_along(partial, "seq", 1) for partial in (low, high)]
    if paired:
        across += [exchanged(after(z, high), "doc", 2) for z in z_blocks]
        parts[1] = after(parts[1], z_blocks[1], z_blocks[2], across[1])

    starts = lax.dynamic_index_in_dim(patch_start, device, 0, keepdims=False)
    ends = jnp.concatenate([starts[1:], jnp.full((1,), nbytes, jnp.int32)])
    row = lambda g: g.astype(jnp.float32)[None, :]
    encoded, pooled = pool(
        (device == 0).astype(jnp.int32)[None], own, lse, parts, row(byte_gain), pool_query,
        starts[:, None], ends[:, None],
    )
    if paired:
        weights = []
        for z, x in zip([mine] + z_blocks, across):
            weights += [z, exchanged(after(z, pooled), "doc", 1), x, exchanged(after(x, pooled), "doc", 1)]
        plan, n_copies = quarter_plan, 3 * len(weights)
    else:
        weights = [lax.all_gather(w, "seq", axis=0, tiled=True) for w in (w_up, w_kv)]
        plan, n_copies = whole_plan, 2

    place = jnp.arange(slots, dtype=jnp.int32)
    own_allowed = (place[None, :] <= place[:, None]) & (starts < nbytes)[None, :]
    if paired:
        zs = [exchanged(pooled, "seq", 2 * j) for j in range(1, 3)]
        zs.append(exchanged(zs[1], "seq", 2))
        ys = [exchanged(b, "seq", 1) for b in [pooled] + zs]
        blocks = [pooled] + zs + ys
        order = jnp.stack([device ^ m for m in (2, 4, 6, 1, 3, 5, 7)])
    else:
        blocks = [pooled, lax.all_gather(pooled, "seq", axis=0, tiled=True)]
        order = jnp.arange(n_seq, dtype=jnp.int32)
    live = (patch_start < nbytes)[order] & (order < device)[:, None]
    allowed = jnp.concatenate(
        [own_allowed, jnp.broadcast_to(live.reshape(1, -1), (slots, live.size))], axis=1
    )
    bias = jnp.where(allowed, 0.0, LOW).astype(jnp.float32)
    at = jnp.stack([device, doc]).astype(jnp.int32)
    byte_out, patch_out = patches(
        at, blocks, weights, plan, n_copies,
        (w_up.shape[0] * n_seq, w_up.shape[1]), (w_kv.shape[0] * n_seq, w_kv.shape[1]),
        encoded, bias, [row(patch_gain), row(out_gain), row(dec_gain)],
        starts[:, None], starts[None, :], w_up.shape[1],
    )
    return (byte_out, patch_out)


def solution(mesh):
    placed = (
        P(("doc", "seq"), None),
        P(("doc", "seq"), None),
        P(("doc", "seq"), None),
        P(),
        P(),
        P("seq", None),
        P(),
        P("seq", None),
        P(),
        P(),
        P("doc", None),
    )
    return jax.shard_map(
        per_device,
        mesh=mesh,
        in_specs=placed,
        out_specs=(P(("doc", "seq"), None), P(("doc", "seq"), None)),
        check_vma=False,
    )
```

```python
import functools

import jax
import jax.numpy as jnp
from jax import lax
from jax.experimental import pallas as pl
from jax.experimental.pallas import tpu as pltpu
from jax.sharding import PartitionSpec as P

PATCH_QUERY_HEADS = 32
PATCH_KEY_HEADS = 8
LOG2E = 1.4426950408889634
LOW = -1e30
TILE = 128
GROUP = 4
epsilon = 1e-06
VMEM = pl.BlockSpec(memory_space=pltpu.VMEM)
SMALL = pl.CostEstimate(flops=1, bytes_accessed=1, transcendentals=0)
ANY = pl.BlockSpec(memory_space=pl.ANY)


def dot_t(a, b):
    return lax.dot_general(a, b, (((1,), (1,)), ((), ())), preferred_element_type=jnp.float32)


def dot(a, b):
    return jnp.dot(a, b, preferred_element_type=jnp.float32)


def split(value):
    high = value.astype(jnp.bfloat16)
    rest = value - high.astype(jnp.float32)
    middle = rest.astype(jnp.bfloat16)
    return high, middle, (rest - middle.astype(jnp.float32)).astype(jnp.bfloat16)


def keep_lse(ref, base, columns_ref, count):
    for start in range(0, columns_ref.shape[0], TILE):
        rows = slice(start, start + TILE)
        across = jnp.transpose(columns_ref[rows, :])[:count, :]
        terms = [term.astype(jnp.float32) for term in split(across)]
        terms.append(jnp.zeros_like(across))
        ref[base:, rows] = jnp.concatenate(terms, axis=0).astype(jnp.bfloat16)


def own_kernel(q_ref, k_ref, v_ref, mix_ref, lse_ref, columns_ref):
    step = pl.program_id(0)
    nbytes, width = q_ref.shape
    size = TILE
    factor = size ** (-0.5) * LOG2E
    row = lax.broadcasted_iota(jnp.int32, (TILE, TILE), 0)
    col = lax.broadcasted_iota(jnp.int32, (TILE, TILE), 1)
    causal = col <= row
    ones = jnp.ones((nbytes, size), jnp.bfloat16)

    for h in range(width // size):
        at = slice(h * size, (h + 1) * size)
        values = jnp.concatenate([v_ref[:, at], ones], axis=1)
        head = step * (width // size) + h
        for start in range(0, nbytes, TILE):
            end = start + TILE
            scores = dot_t(q_ref[start:end, at], k_ref[:end, at])
            last = jnp.where(causal, scores[:, start:end], LOW)
            scores = last if start == 0 else jnp.concatenate([scores[:, :start], last], axis=1)
            peak = jnp.max(scores, axis=1, keepdims=True)
            expo = jnp.exp2((scores - peak) * factor).astype(jnp.bfloat16)
            total = dot(expo, values[:end])
            mix_ref[start:end, at] = (total[:, :size] / total[:, size:]).astype(jnp.bfloat16)
            lse = peak * factor + jnp.log2(total[:, size:])
            columns_ref[start:end, :] = jnp.where(col == head, lse, columns_ref[start:end, :])

    @pl.when(step == pl.num_programs(0) - 1)
    def _():
        keep_lse(lse_ref, 0, columns_ref, lse_ref.shape[0] // 4)


def own_attention(q, k, v):
    nbytes, width = q.shape
    block = pl.BlockSpec((nbytes, GROUP * TILE), lambda h: (0, h))
    rows = (4 * (width // TILE), nbytes)
    return pl.pallas_call(
        functools.partial(own_kernel),
        grid=(width // TILE // GROUP,),
        in_specs=[block] * 3,
        out_specs=[block, pl.BlockSpec(rows, lambda h: (0, 0))],
        out_shape=[
            jax.ShapeDtypeStruct((nbytes, width), jnp.bfloat16),
            jax.ShapeDtypeStruct(rows, jnp.bfloat16),
        ],
        scratch_shapes=[pltpu.VMEM((nbytes, TILE), jnp.float32)],
        cost_estimate=SMALL,
        compiler_params=pltpu.CompilerParams(vmem_limit_bytes=24 * 2**20),
        name="own_attention",
    )(q, k, v)


def cross_kernel(steps, q_ref, k_ref, v_ref, out_ref, columns_ref):
    step = pl.program_id(0)
    nbytes, width = q_ref.shape
    size = TILE
    factor = size ** (-0.5) * LOG2E
    row = lax.broadcasted_iota(jnp.int32, (TILE, TILE), 0)
    col = lax.broadcasted_iota(jnp.int32, (TILE, TILE), 1)
    ones = jnp.ones((nbytes, size), jnp.bfloat16)

    for h in range(width // size):
        at = slice(h * size, (h + 1) * size)
        values = jnp.concatenate([v_ref[:, at], ones], axis=1)
        head = step * (width // size) + h
        columns = pl.ds(pl.multiple_of(head * size, size), size)
        for start in range(0, nbytes, TILE):
            end = start + TILE
            scores = dot_t(q_ref[start:end, at], k_ref[start:, at])
            first = jnp.where(col > row, scores[:, :TILE], LOW)
            scores = jnp.concatenate([first, scores[:, TILE:]], axis=1) if end < nbytes else first
            peak = jnp.max(scores, axis=1, keepdims=True)
            expo = jnp.exp2((scores - peak) * factor)
            if end == nbytes:
                expo = jnp.where(col > row, expo, 0.0)
            total = dot(expo.astype(jnp.bfloat16), values[start:])
            norm = total[:, size:]
            some = norm > 0
            norm = jnp.where(some, norm, 1.0)
            out_ref[start:end, columns] = (total[:, :size] / norm).astype(jnp.bfloat16)
            lse = jnp.where(some, peak * factor + jnp.log2(norm), LOW)
            columns_ref[start:end, :] = jnp.where(col == head, lse, columns_ref[start:end, :])

    @pl.when(step == steps - 1)
    def _():
        keep_lse(out_ref, nbytes, columns_ref, steps * (width // size))


def cross_attention(q, k, v, first, count):
    nbytes, width = q.shape
    size = GROUP * TILE
    block = pl.BlockSpec((nbytes, size), lambda h: (0, h + first // GROUP))
    out = (nbytes + 4 * count, count * TILE)
    return pl.pallas_call(
        functools.partial(cross_kernel, count // GROUP),
        grid=(count // GROUP,),
        in_specs=[pl.BlockSpec((nbytes, size), lambda h: (0, h)), block, block],
        out_specs=pl.BlockSpec(out, lambda h: (0, 0)),
        out_shape=jax.ShapeDtypeStruct(out, jnp.bfloat16),
        scratch_shapes=[pltpu.VMEM((nbytes, TILE), jnp.float32)],
        cost_estimate=SMALL,
        compiler_params=pltpu.CompilerParams(vmem_limit_bytes=24 * 2**20),
        name="cross_attention",
    )(q, k, v)


def spread(terms, first, count):
    n = terms.shape[0] // 4
    row = lax.broadcasted_iota(jnp.int32, (4 * n, count * TILE), 0)
    col = lax.broadcasted_iota(jnp.int32, (4 * n, count * TILE), 1) // TILE + first
    one = jnp.where((row % n == col) & (row < 3 * n), 1.0, 0.0).astype(jnp.bfloat16)
    return lax.dot_general(terms, one, (((0,), (0,)), ((), ())), preferred_element_type=jnp.float32)


def pool_kernel(
    lead_ref, own_ref, lse_ref, *refs
):
    *part_refs, gain_ref, query_ref, start_ref, next_ref, enc_ref, pooled_ref = refs
    nbytes, width = own_ref.shape
    slots = start_ref.shape[0]
    size = TILE
    factor = size ** (-0.5) * LOG2E
    leading = lead_ref[0] != 0
    for start in range(0, nbytes, TILE):
        rows = slice(start, start + TILE)
        mixes = []
        squares = jnp.zeros((TILE, size), jnp.float32)
        first = 0
        for part_ref in part_refs:
            count = part_ref.shape[1] // TILE
            own_lse = spread(lse_ref[:, rows], first, count)
            part_lse = spread(part_ref[nbytes:, rows], 0, count)
            for h in range(count):
                at = slice(h * size, (h + 1) * size)
                gap = jnp.where(leading, LOW, part_lse[:, at] - own_lse[:, at])
                share = 1.0 / (1.0 + jnp.exp2(gap))
                own = own_ref[rows, (first + h) * size : (first + h + 1) * size].astype(jnp.float32)
                part = part_ref[rows, at].astype(jnp.float32)
                mix = part + (own - part) * share
                squares += mix * mix
                mixes.append(mix)
            first += count
        scale = lax.rsqrt(jnp.sum(squares, axis=1, keepdims=True) / width + epsilon)
        for h, mix in enumerate(mixes):
            at = slice(h * size, (h + 1) * size)
            enc_ref[rows, at] = (mix * scale * gain_ref[:, at]).astype(jnp.bfloat16)
    enc = enc_ref[...]
    n_heads = query_ref.shape[0]
    wide = jnp.concatenate([query_ref[...].astype(jnp.float32)] * n_heads, axis=1)
    head_row = lax.broadcasted_iota(jnp.int32, wide.shape, 0)
    head_col = lax.broadcasted_iota(jnp.int32, wide.shape, 1) // size
    wide = jnp.where(head_row == head_col, wide, 0.0).astype(jnp.bfloat16)
    scores = dot_t(wide, enc) * factor
    place = lax.broadcasted_iota(jnp.int32, (slots, nbytes), 1)
    member = (place >= start_ref[...]) & (place < next_ref[...])
    for h in range(n_heads):
        inside = jnp.where(member, scores[h : h + 1, :], LOW)
        peak = jnp.max(inside, axis=1, keepdims=True)
        expo = jnp.where(member, jnp.exp2(inside - peak), 0.0)
        total = jnp.sum(expo, axis=1, keepdims=True)
        weights = (expo * jnp.where(total > 0, 1.0 / total, 0.0)).astype(jnp.bfloat16)
        pooled_ref[:, h * size : (h + 1) * size] = dot(
            weights, enc[:, h * size : (h + 1) * size]
        ).astype(jnp.bfloat16)


def pool(leading, own, lse, parts, gain, pool_query, starts, ends):
    nbytes, width = own.shape
    slots = starts.shape[0]
    return pl.pallas_call(
        pool_kernel,
        in_specs=[pl.BlockSpec(memory_space=pltpu.SMEM)] + [VMEM] * (len(parts) + 6),
        out_specs=[VMEM, VMEM],
        out_shape=[
            jax.ShapeDtypeStruct((nbytes, width), jnp.bfloat16),
            jax.ShapeDtypeStruct((slots, width), jnp.bfloat16),
        ],
        cost_estimate=SMALL,
        compiler_params=pltpu.CompilerParams(vmem_limit_bytes=32 * 2**20),
        name="pool",
    )(leading, own, lse, *parts, gain, pool_query, starts, ends)


def patch_kernel(n_blocks, plan, n_weights, at_ref, *refs):
    blocks = refs[:n_blocks]
    weights = refs[n_blocks : n_blocks + n_weights]
    (
        enc_ref, bias_ref, pgain_ref, ogain_ref, dgain_ref, start_col_ref, start_row_ref,
        byte_ref, patch_ref, all_ref, up_ref, kv_w_ref, kv_ref, mix_ref, in_ref, sems,
    ) = refs[n_blocks + n_weights :]
    ups, kvs = plan(at_ref, weights, up_ref, kv_w_ref)
    ups = [pltpu.make_async_copy(*copy, sems.at[i]) for i, copy in enumerate(ups)]
    kvs = [pltpu.make_async_copy(*copy, sems.at[len(ups) + i]) for i, copy in enumerate(kvs)]
    for copy in ups:
        copy.start()

    slots = patch_ref.shape[0]
    offset = 0
    for block in blocks:
        all_ref[offset : offset + block.shape[0], :] = block[...]
        offset += block.shape[0]
    step = 4 * slots
    for copy in ups:
        copy.wait()
    for copy in kvs:
        copy.start()
    for r in range(0, offset, step):
        rows = slice(r, min(r + step, offset))
        lifted = dot(all_ref[rows, :], up_ref[...])
        scale = lax.rsqrt(jnp.mean(lifted * lifted, axis=1, keepdims=True) + epsilon)
        in_ref[rows, :] = (lifted * scale * pgain_ref[...]).astype(jnp.bfloat16)
    for copy in kvs:
        copy.wait()
    for r in range(0, offset, step):
        rows = slice(r, min(r + step, offset))
        kv_ref[rows, :] = dot(in_ref[rows, :], kv_w_ref[...]).astype(jnp.bfloat16)

    size = patch_ref.shape[1] // PATCH_QUERY_HEADS
    rows = kv_ref.shape[0]
    half_width = PATCH_KEY_HEADS * size
    factor = size ** (-0.5) * LOG2E
    groups = PATCH_QUERY_HEADS // PATCH_KEY_HEADS
    pair = 2 * size
    lane_half = lax.broadcasted_iota(jnp.int32, (slots, pair), 1) // size
    ones = jnp.ones((rows, pair), jnp.bfloat16)
    for kp in range(PATCH_KEY_HEADS // 2):
        keys = kv_ref[:, kp * pair : (kp + 1) * pair]
        values = jnp.concatenate(
            [kv_ref[:, half_width + kp * pair : half_width + (kp + 1) * pair], ones], axis=1
        )
        for half in range(2):
            first = (2 * kp + half) * groups
            queries = []
            for g in range(groups):
                at = (first + g) // 2 * pair
                q = in_ref[:slots, at : at + pair].astype(jnp.float32)
                if g % 2 != half:
                    q = pltpu.roll(q, size, 1)
                queries.append(jnp.where(lane_half == half, q, 0.0).astype(jnp.bfloat16))
            scores = dot_t(jnp.concatenate(queries, axis=0), keys)
            outs = []
            for g in range(groups):
                part = scores[g * slots : (g + 1) * slots, :] * factor + bias_ref[...]
                peak = jnp.max(part, axis=1, keepdims=True)
                outs.append(jnp.exp2(part - peak).astype(jnp.bfloat16))
            total = dot(jnp.concatenate(outs, axis=0), values)
            mixed = total[:, :pair] / total[:, pair:]
            for g in range(0, groups, 2):
                two = [mixed[(g + i) * slots : (g + i + 1) * slots, :] for i in range(2)]
                two = [t if i == half else pltpu.roll(t, size, 1) for i, t in enumerate(two)]
                at = (first + g) // 2 * pair
                mix_ref[:, at : at + pair] = jnp.where(lane_half == 0, two[0], two[1])

    nbytes = enc_ref.shape[0]
    mix = mix_ref[...]
    scale = lax.rsqrt(jnp.mean(mix * mix, axis=1, keepdims=True) + epsilon)
    alive = jnp.where(start_col_ref[...] < nbytes, 1.0, 0.0)
    patch_ref[...] = (mix * scale * ogain_ref[...] * alive).astype(jnp.bfloat16)

    width = enc_ref.shape[1]
    size = TILE
    factor = size ** (-0.5) * LOG2E
    ones = jnp.ones((slots, size), jnp.bfloat16)
    for start in range(0, nbytes, 512):
        place = lax.broadcasted_iota(jnp.int32, (512, slots), 0) + start
        allowed = start_row_ref[...] <= place
        crosses = []
        squares = jnp.zeros((512, size), jnp.float32)
        for h in range(width // size):
            scores = dot_t(
                enc_ref[start : start + 512, h * size : (h + 1) * size],
                patch_ref[:, 2 * h * size : (2 * h + 1) * size],
            )
            scores = jnp.where(allowed, scores * factor, LOW)
            peak = jnp.max(scores, axis=1, keepdims=True)
            expo = jnp.exp2(scores - peak).astype(jnp.bfloat16)
            values = jnp.concatenate(
                [patch_ref[:, (2 * h + 1) * size : (2 * h + 2) * size], ones], axis=1
            )
            total = dot(expo, values)
            cross = total[:, :size] / total[:, size:]
            squares += cross * cross
            crosses.append(cross)
        scale = lax.rsqrt(jnp.sum(squares, axis=1, keepdims=True) / width + epsilon)
        for h, cross in enumerate(crosses):
            at = h * size
            byte_ref[start : start + 512, at : at + size] = (
                cross * scale * dgain_ref[:, at : at + size]
            ).astype(jnp.bfloat16)


def patches(at, blocks, weights, plan, n_copies, up_shape, kv_shape, encoded, bias, gains, starts_col, starts_row, n_patch_width):
    rows = sum(b.shape[0] for b in blocks)
    slots = starts_col.shape[0]
    return pl.pallas_call(
        functools.partial(patch_kernel, len(blocks), plan, len(weights)),
        in_specs=[pl.BlockSpec(memory_space=pltpu.SMEM)]
        + [VMEM] * len(blocks)
        + [ANY] * len(weights)
        + [VMEM] * 7,
        out_specs=[VMEM, VMEM],
        out_shape=[
            jax.ShapeDtypeStruct(encoded.shape, jnp.bfloat16),
            jax.ShapeDtypeStruct((slots, n_patch_width), jnp.bfloat16),
        ],
        scratch_shapes=[
            pltpu.VMEM((rows, up_shape[0]), jnp.bfloat16),
            pltpu.VMEM(up_shape, jnp.bfloat16),
            pltpu.VMEM(kv_shape, jnp.bfloat16),
            pltpu.VMEM((rows, kv_shape[1]), jnp.bfloat16),
            pltpu.VMEM((slots, n_patch_width), jnp.float32),
            pltpu.VMEM((rows, n_patch_width), jnp.bfloat16),
            pltpu.SemaphoreType.DMA((n_copies,)),
        ],
        cost_estimate=SMALL,
        compiler_params=pltpu.CompilerParams(vmem_limit_bytes=48 * 2**20),
        name="patches",
    )(at, *blocks, *weights, encoded, bias, *gains, starts_col, starts_row)


def exchanged(value, axis, mask):
    return lax.ppermute(value, axis, [(i, i ^ mask) for i in range(lax.axis_size(axis))])


def passed_along(value, axis, steps):
    count = lax.axis_size(axis)
    pairs = [(i, i + steps) for i in range(count) if 0 <= i + steps < count]
    return lax.ppermute(value, axis, pairs)


def whole_plan(at_ref, weights, up_ref, kv_ref):
    return [(weights[0], up_ref)], [(weights[1], kv_ref)]


def quarter_plan(at_ref, weights, up_ref, kv_ref):
    z, doc = at_ref[0] // 2, at_ref[1]
    up_rows, up_cols = up_ref.shape[0] // 4, up_ref.shape[1] // 4
    kv_rows, kv_cols = kv_ref.shape[0] // 8, kv_ref.shape[1] // 4
    ups, kvs = [], []
    for i, ref in enumerate(weights):
        block, part = i // 4, i % 4
        zb, q = z ^ block, doc ^ part
        cols = pl.ds(pl.multiple_of(q * up_cols, up_cols), up_cols)
        rows = pl.ds(pl.multiple_of(zb * up_rows, up_rows), up_rows)
        ups.append((ref.at[:up_rows, :], up_ref.at[rows, cols]))
        cols = pl.ds(pl.multiple_of(q * kv_cols, kv_cols), kv_cols)
        for y in range(2):
            rows = pl.ds(pl.multiple_of((2 * zb + y) * kv_rows, kv_rows), kv_rows)
            kvs.append((ref.at[up_rows:, y * kv_cols : (y + 1) * kv_cols], kv_ref.at[rows, cols]))
    return ups, kvs


def paired_weights(w_up, w_kv):
    doc = lax.axis_index("doc")
    y = lax.axis_index("seq") % 2
    up = lax.dynamic_slice_in_dim(w_up, doc * (w_up.shape[1] // 4), w_up.shape[1] // 4, 1)
    kv = lax.dynamic_slice_in_dim(w_kv, doc * (w_kv.shape[1] // 4), w_kv.shape[1] // 4, 1)
    n = up.shape[0]
    piece = jnp.concatenate([up, jnp.concatenate([kv[:n], kv[n:]], axis=1)], axis=0)
    other = exchanged(piece, "seq", 1)
    low, high = jnp.where(y == 0, piece, other), jnp.where(y == 0, other, piece)

    def unpacked(p):
        w = p.shape[1] // 2
        return jnp.concatenate([p[n:, :w], p[n:, w:]], axis=0)

    mine = jnp.concatenate(
        [low[:n], high[:n], jnp.concatenate([unpacked(low), unpacked(high)], axis=1)], axis=0
    )
    return mine, other


def after(value, *others):
    return lax.optimization_barrier((value,) + others)[0]


def per_device(
    byte_q, byte_k, byte_v, byte_gain, pool_query, w_up, patch_gain, w_kv, out_gain, dec_gain,
    patch_start,
):
    nbytes = byte_q.shape[0]
    slots = patch_start.shape[1]
    device = lax.axis_index("seq")
    doc = lax.axis_index("doc")
    n_seq, n_doc = lax.axis_size("seq"), lax.axis_size("doc")
    paired = n_seq == 8 and n_doc == 4

    count = byte_q.shape[1] // TILE // 2
    halves = [byte_q[:, i * count * TILE : (i + 1) * count * TILE] for i in range(2)]
    if paired:
        mine, other = paired_weights(w_up, w_kv)
        halves = [after(h, other) for h in halves]
        byte_q = after(byte_q, other)
    q_next = [passed_along(h, "seq", -1) for h in halves]
    if paired:
        z_blocks = [exchanged(mine, "seq", 2 * j) for j in (1, 2)]
        z_blocks.append(exchanged(z_blocks[1], "seq", 2))
        across = [exchanged(mine, "doc", 2)]
    own, lse = own_attention(byte_q, byte_k, byte_v)
    first = [lse] + (across[:1] if paired else [])
    low = cross_attention(after(q_next[0], *first), byte_k, byte_v, 0, count)
    second = [low]
    high = cross_attention(after(q_next[1], *second), byte_k, byte_v, count, count)
    parts = [passed_along(partial, "seq", 1) for partial in (low, high)]
    if paired:
        across += [exchanged(after(z, high), "doc", 2) for z in z_blocks]
        parts[1] = after(parts[1], z_blocks[1], across[1])

    starts = lax.dynamic_index_in_dim(patch_start, device, 0, keepdims=False)
    ends = jnp.concatenate([starts[1:], jnp.full((1,), nbytes, jnp.int32)])
    row = lambda g: g.astype(jnp.float32)[None, :]
    encoded, pooled = pool(
        (device == 0).astype(jnp.int32)[None], own, lse, parts, row(byte_gain), pool_query,
        starts[:, None], ends[:, None],
    )
    if paired:
        weights = []
        for z, x in zip([mine] + z_blocks, across):
            weights += [z, exchanged(after(z, pooled), "doc", 1), x, exchanged(after(x, pooled), "doc", 1)]
        plan, n_copies = quarter_plan, 3 * len(weights)
    else:
        weights = [lax.all_gather(w, "seq", axis=0, tiled=True) for w in (w_up, w_kv)]
        plan, n_copies = whole_plan, 2

    place = jnp.arange(slots, dtype=jnp.int32)
    own_allowed = (place[None, :] <= place[:, None]) & (starts < nbytes)[None, :]
    if paired:
        zs = [exchanged(pooled, "seq", 2 * j) for j in range(1, 3)]
        zs.append(exchanged(zs[1], "seq", 2))
        ys = [exchanged(b, "seq", 1) for b in [pooled] + zs]
        blocks = [pooled] + zs + ys
        order = jnp.stack([device ^ m for m in (2, 4, 6, 1, 3, 5, 7)])
    else:
        blocks = [pooled, lax.all_gather(pooled, "seq", axis=0, tiled=True)]
        order = jnp.arange(n_seq, dtype=jnp.int32)
    live = (patch_start < nbytes)[order] & (order < device)[:, None]
    allowed = jnp.concatenate(
        [own_allowed, jnp.broadcast_to(live.reshape(1, -1), (slots, live.size))], axis=1
    )
    bias = jnp.where(allowed, 0.0, LOW).astype(jnp.float32)
    at = jnp.stack([device, doc]).astype(jnp.int32)
    byte_out, patch_out = patches(
        at, blocks, weights, plan, n_copies,
        (w_up.shape[0] * n_seq, w_up.shape[1]), (w_kv.shape[0] * n_seq, w_kv.shape[1]),
        encoded, bias, [row(patch_gain), row(out_gain), row(dec_gain)],
        starts[:, None], starts[None, :], w_up.shape[1],
    )
    return (byte_out, patch_out)


def solution(mesh):
    placed = (
        P(("doc", "seq"), None),
        P(("doc", "seq"), None),
        P(("doc", "seq"), None),
        P(),
        P(),
        P("seq", None),
        P(),
        P("seq", None),
        P(),
        P(),
        P("doc", None),
    )
    return jax.shard_map(
        per_device,
        mesh=mesh,
        in_specs=placed,
        out_specs=(P(("doc", "seq"), None), P(("doc", "seq"), None)),
        check_vma=False,
    )
```
